128 devices in a mesh: section: 2 (over core), seq: 8 (over y, x_lo), mp: 8 (over x_hi, z).
Axes of the slice: x: 4 (x_hi: 2, x_lo: 2; x = x_hi * 2 + x_lo), y: 4, z: 4, core: 2. Of those that a mesh axis runs over, the one named last changes fastest.
Arguments:
- bottleneck: bfloat16 [2, 1024, 4096], P('section', ('seq', 'mp')), may hold values from -6 to 6
- qkv_weight: bfloat16 [3, 4096, 4096], P(None, None, ('section', 'mp')), may hold values from -0.2 to 0.2
- out_weight: bfloat16 [4096, 4096], P(('section', 'mp')), may hold values from -0.5 to 0.5
- up_weight: bfloat16 [4096, 16384], P(None, ('section', 'mp')), may hold values from -0.09375 to 0.09375
- down_weight: bfloat16 [16384, 4096], P(('section', 'mp')), may hold values from -0.046875 to 0.046875
- cotangent: bfloat16 [2, 1024, 4096], P('section', ('seq', 'mp')), may hold values from -6 to 6
Outputs:
- block_out: bfloat16 [2, 1024, 4096], P('section', ('seq', 'mp'))
- grad_input: bfloat16 [2, 1024, 4096], P('section', ('seq', 'mp'))
The draws below stay inside these ranges and needn't reach their ends.
All inputs are finite; a program needn't handle non-finite values.
Results may differ from the reference program's by a relative error of at most 0.025.
Values may be sent and summed in bfloat16 or wider, within the bound.
No kernel may reach another device: no remote copies, remote signals or barrier semaphores. Data moves between devices by JAX's collectives and lax.ppermute only.
A program may use at most 128 MiB of HBM per device.

```python
import math
import jax
import jax.numpy as jnp
from jax import lax

D = 4096
H = 32
HD = 128
FF = 16384
LEN = 1024
IMAGES = 2


def draw_qkv_weight(key, part):
    first, second, third = jax.random.split(key, 3)
    spread = D ** (-0.5)
    query_part = jax.random.normal(first, (D, H * HD)) * spread
    key_part = jax.random.normal(second, (D, H * HD)) * spread
    value_part = jax.random.normal(third, (D, H * HD)) * spread
    stacked = jnp.stack([query_part, key_part, value_part]).astype(jnp.float32)
    return jnp.clip(stacked, -0.19921875, 0.19921875).astype(jnp.bfloat16)


def shard_levels(own_key, dims, shards, low, top_value):
    level = 1.0
    for dim, parts in shards:
        draws = jax.random.uniform(jax.random.fold_in(jax.random.fold_in(own_key, 6), dim), (parts,), jnp.float32, low / len(shards), top_value / len(shards))
        level = level * jnp.repeat(jnp.exp(draws), dims[dim] // parts).reshape((-1,) + (1,) * (len(dims) - 1 - dim))
    return level


def gaussian(rng, dims, scale, reach, shards=(), kind=jnp.bfloat16):
    level = shard_levels(rng, dims, shards, -0.22, 0.18) if shards else 1.0
    drawn = jax.random.normal(rng, dims, jnp.float32) * scale * level
    return jnp.minimum(jnp.maximum(drawn, -reach), reach).astype(kind)


def setup_inputs(seed: int = 0) -> dict:
    seeds = jax.random.split(jax.random.key(seed), 7)
    return {
        "bottleneck": gaussian(seeds[0], (IMAGES, LEN, D), 1.0, 6.0, ((0, 2), (1, 64))),
        "qkv_weight": draw_qkv_weight(jax.random.fold_in(seeds[6], 71), 0),
        "out_weight": gaussian(seeds[2], (H * HD, D), HD ** -0.5, 0.5, ((0, 16),)),
        "up_weight": gaussian(seeds[3], (D, FF), D ** -0.5, 0.09375, ((1, 16),)),
        "down_weight": gaussian(seeds[4], (FF, D), FF ** -0.5, 0.046875, ((0, 16),)),
        "cotangent": gaussian(seeds[5], (IMAGES, LEN, D), 1.0, 6.0, ((0, 2), (1, 64))),
    }


norm_eps = 1e-06

def layer_norm(inputs):
    row_mean = lax.optimization_barrier(jnp.mean(inputs, axis=-1, keepdims=True))
    centered = inputs - row_mean
    inv_std = lax.rsqrt(lax.optimization_barrier(jnp.mean(centered * centered, axis=-1, keepdims=True)) + norm_eps)
    return (centered * inv_std, inv_std)

def norm_backward(normed, inv_std, grad_in):
    mean_grad = lax.optimization_barrier(jnp.mean(grad_in, axis=-1, keepdims=True))
    mean_mix = lax.optimization_barrier(jnp.mean(grad_in * normed, axis=-1, keepdims=True))
    return inv_std * (grad_in - mean_grad - normed * mean_mix)

def gelu_value(pre_act):
    return pre_act * 0.5 * (1.0 + lax.erf(pre_act * 0.7071067811865476))

def gelu_slope(pre_act):
    cumul = 0.5 * (1.0 + lax.erf(pre_act * 0.7071067811865476))
    return cumul + pre_act * jnp.exp(-0.5 * pre_act * pre_act) * 0.3989422804014327

def to_float(array_low):
    return lax.optimization_barrier(array_low).astype(jnp.float32)

def reference(bottleneck, qkv_weight, out_weight, up_weight, down_weight, cotangent):
    images, length, model_width = bottleneck.shape
    score_scale = 1.0 / math.sqrt(HD)
    total_rows = images * length
    flat_rows = bottleneck.reshape(total_rows, model_width).astype(jnp.float32)
    normed_one, inv_one = layer_norm(flat_rows)
    normed_low = normed_one.astype(jnp.bfloat16)
    projected = [jnp.dot(normed_low, qkv_weight[slot_index], preferred_element_type=jnp.float32).astype(jnp.bfloat16) for slot_index in range(3)]

    def to_heads(flat_data):
        return flat_data.reshape(images, length, H, HD).transpose(2, 0, 1, 3)

    def from_heads(per_head):
        return per_head.transpose(1, 2, 0, 3).reshape(total_rows, H * HD)
    queries, key_rows, value_rows = [to_heads(matrix_rows) for matrix_rows in projected]

    def head_scores(head_q, head_k):
        return jnp.einsum('ild,imd->ilm', head_q.astype(jnp.float32), head_k.astype(jnp.float32)) * score_scale

    def forward_head(operands):
        head_q, head_k, head_v = operands
        scores = head_scores(head_q, head_k)
        row_max = lax.optimization_barrier(jnp.max(scores, axis=-1, keepdims=True))
        weights = jnp.exp(scores - row_max)
        totals = lax.optimization_barrier(jnp.sum(weights, axis=-1, keepdims=True))
        mixed_values = jnp.einsum('ilm,imd->ild', to_float(weights.astype(jnp.bfloat16)), head_v.astype(jnp.float32)) / totals
        return (mixed_values.astype(jnp.bfloat16), (row_max + jnp.log(totals))[..., 0])
    attended_heads, log_total = lax.map(forward_head, (queries, key_rows, value_rows))
    attended = from_heads(attended_heads)
    attn_sum = jnp.dot(attended, out_weight, preferred_element_type=jnp.float32)
    resid = (flat_rows + attn_sum).astype(jnp.bfloat16)
    normed_two, inv_two = layer_norm(resid.astype(jnp.float32))
    hidden_pre = jnp.dot(normed_two.astype(jnp.bfloat16), up_weight, preferred_element_type=jnp.float32)
    hidden = gelu_value(hidden_pre).astype(jnp.bfloat16)
    ffn_sum = jnp.dot(hidden, down_weight, preferred_element_type=jnp.float32)
    block_out = (resid.astype(jnp.float32) + ffn_sum).astype(jnp.bfloat16)
    grad_rows = cotangent.reshape(total_rows, model_width)
    grad_act = jnp.dot(grad_rows, down_weight.T, preferred_element_type=jnp.float32)
    grad_hidden = (grad_act * gelu_slope(hidden_pre)).astype(jnp.bfloat16)
    grad_norm_two = jnp.dot(grad_hidden, up_weight.T, preferred_element_type=jnp.float32)
    grad_resid = (grad_rows.astype(jnp.float32) + norm_backward(normed_two, inv_two, grad_norm_two)).astype(jnp.bfloat16)
    grad_attn = jnp.dot(grad_resid, out_weight.T, preferred_element_type=jnp.float32).astype(jnp.bfloat16)
    grad_attn_heads = to_heads(grad_attn)

    def backward_head(operands):
        head_q, head_k, head_v, head_o, head_do, head_lse = operands
        scores = head_scores(head_q, head_k)
        prob_rows = jnp.exp(scores - head_lse[..., None])
        row_delta = lax.optimization_barrier(jnp.sum(head_do.astype(jnp.float32) * head_o.astype(jnp.float32), axis=-1, keepdims=True))
        grad_probs = jnp.einsum('ild,imd->ilm', head_do.astype(jnp.float32), head_v.astype(jnp.float32))
        grad_scores = to_float((prob_rows * (grad_probs - row_delta) * score_scale).astype(jnp.bfloat16))
        grad_query = jnp.einsum('ilm,imd->ild', grad_scores, head_k.astype(jnp.float32)).astype(jnp.bfloat16)
        grad_key = jnp.einsum('ilm,ild->imd', grad_scores, head_q.astype(jnp.float32)).astype(jnp.bfloat16)
        prob_low = to_float(prob_rows.astype(jnp.bfloat16))
        grad_value = jnp.einsum('ilm,ild->imd', prob_low, head_do.astype(jnp.float32)).astype(jnp.bfloat16)
        return (grad_query, grad_key, grad_value)
    grad_q, grad_k, grad_v = lax.map(backward_head, (queries, key_rows, value_rows, attended_heads, grad_attn_heads, log_total))
    grad_norm_one = jnp.dot(from_heads(grad_q), qkv_weight[0].T, preferred_element_type=jnp.float32)
    grad_norm_one = grad_norm_one + jnp.dot(from_heads(grad_k), qkv_weight[1].T, preferred_element_type=jnp.float32)
    grad_norm_one = grad_norm_one + jnp.dot(from_heads(grad_v), qkv_weight[2].T, preferred_element_type=jnp.float32)
    grad_input = (grad_resid.astype(jnp.float32) + norm_backward(normed_one, inv_one, grad_norm_one)).astype(jnp.bfloat16)
    return (block_out.reshape(bottleneck.shape), grad_input.reshape(bottleneck.shape))
```

```python
import math

import jax
import jax.numpy as jnp
from jax import lax
from jax.sharding import PartitionSpec as P

HD = 128


norm_eps = 1e-06


def layer_norm(inputs):
    row_mean = jnp.mean(inputs, axis=-1, keepdims=True)
    centered = inputs - row_mean
    inv_std = lax.rsqrt(jnp.mean(centered * centered, axis=-1, keepdims=True) + norm_eps)
    return (centered * inv_std, inv_std)


def norm_backward(normed, inv_std, grad_in):
    mean_grad = jnp.mean(grad_in, axis=-1, keepdims=True)
    mean_mix = jnp.mean(grad_in * normed, axis=-1, keepdims=True)
    return inv_std * (grad_in - mean_grad - normed * mean_mix)


def gelu_value(pre_act):
    return pre_act * 0.5 * (1.0 + lax.erf(pre_act * 0.7071067811865476))


def gelu_slope(pre_act):
    cumul = 0.5 * (1.0 + lax.erf(pre_act * 0.7071067811865476))
    return cumul + pre_act * jnp.exp(-0.5 * pre_act * pre_act) * 0.3989422804014327


def swap_section(data):
    return lax.ppermute(data, "section", [(0, 1), (1, 0)])


def spread(own, axis):
    size = lax.axis_size(axis)
    copies = jnp.broadcast_to(own[None], (size,) + own.shape)
    return lax.all_to_all(copies, axis, 0, 0)


def gather_rows(own):
    mine = spread(own, "mp").reshape(-1, own.shape[-1])
    return jnp.concatenate([mine, swap_section(mine)], axis=0)


def scatter_rows(partial):
    half = partial.shape[0] // 2
    width = partial.shape[1]
    other = swap_section(partial[half:].astype(jnp.bfloat16))
    pair = (partial[:half] + other.astype(jnp.float32)).astype(jnp.bfloat16)
    size = lax.axis_size("mp")
    parts = lax.all_to_all(pair.reshape(size, half // size, width), "mp", 0, 0)
    return jnp.sum(parts.astype(jnp.float32), axis=0)


def scatter_rows_later(partial):
    half = partial.shape[0] // 2
    other = swap_section(partial[half:].astype(jnp.bfloat16))
    pair = (partial[:half] + other.astype(jnp.float32)).astype(jnp.bfloat16)
    return lax.psum_scatter(pair, "mp", scatter_dimension=0, tiled=True).astype(jnp.float32)


def gather_rows_early(own):
    mine = lax.all_gather(own, "mp", axis=0, tiled=True)
    return jnp.concatenate([mine, swap_section(mine)], axis=0)


def dot_f32(lhs, rhs):
    return jnp.dot(lhs, rhs, preferred_element_type=jnp.float32)


def dot_nt(lhs, rhs):
    return jnp.einsum("tf,df->td", lhs, rhs, preferred_element_type=jnp.float32)


def per_device(bottleneck, qkv_weight, out_weight, up_weight, down_weight, cotangent):
    own_in = bottleneck[0].astype(jnp.float32)
    own_cot = cotangent[0]
    images = 2
    head_cols = qkv_weight.shape[2]
    head_count = head_cols // HD
    score_scale = 1.0 / math.sqrt(HD)

    cot_all = gather_rows_early(own_cot)
    normed_one, inv_one = layer_norm(own_in)
    normed_all = gather_rows(normed_one.astype(jnp.bfloat16))
    total_rows = normed_all.shape[0]
    block_rows = total_rows // images
    projected = jnp.einsum(
        "td,kdf->ktf", normed_all, qkv_weight, preferred_element_type=jnp.float32
    ).astype(jnp.bfloat16)
    query_heads = projected[0].reshape(images, block_rows, head_count, HD)
    pairs = spread(projected[1:].reshape(2, images, block_rows, head_cols), "seq")
    seq_size = pairs.shape[0]
    length = seq_size * block_rows
    heads = jnp.transpose(pairs, (1, 2, 0, 3, 4)).reshape(2, images, length, head_count, HD)
    key_heads, value_heads = heads[0], heads[1]

    scores = (
        jnp.einsum("ilhd,imhd->ihlm", query_heads, key_heads, preferred_element_type=jnp.float32)
        * score_scale
    )
    row_max = jnp.max(scores, axis=-1)
    weights = jnp.exp(scores - row_max[..., None])
    totals = jnp.sum(weights, axis=-1)
    log_total = row_max + jnp.log(totals)
    mixed_values = jnp.einsum(
        "ihlm,imhd->ilhd",
        weights.astype(jnp.bfloat16),
        value_heads,
        preferred_element_type=jnp.float32,
    )
    attended = (mixed_values / jnp.transpose(totals, (0, 2, 1))[..., None]).astype(jnp.bfloat16)
    attn_own = scatter_rows(dot_f32(attended.reshape(total_rows, head_cols), out_weight))
    resid = (own_in + attn_own).astype(jnp.bfloat16)
    normed_two, inv_two = layer_norm(resid.astype(jnp.float32))
    normed_two_all = gather_rows(normed_two.astype(jnp.bfloat16))
    hidden_pre = dot_f32(normed_two_all, up_weight)
    hidden = gelu_value(hidden_pre).astype(jnp.bfloat16)
    grad_act = dot_nt(cot_all, down_weight)
    grad_hidden = (grad_act * gelu_slope(hidden_pre)).astype(jnp.bfloat16)
    grad_norm_two = scatter_rows(dot_nt(grad_hidden, up_weight))
    ffn_own = scatter_rows_later(dot_f32(hidden, down_weight))
    block_out = (resid.astype(jnp.float32) + ffn_own).astype(jnp.bfloat16)

    grad_resid = (
        own_cot.astype(jnp.float32) + norm_backward(normed_two, inv_two, grad_norm_two)
    ).astype(jnp.bfloat16)
    grad_resid_all = gather_rows(grad_resid)
    grad_attn = dot_nt(grad_resid_all, out_weight).astype(jnp.bfloat16)
    grad_attn_heads = grad_attn.reshape(images, block_rows, head_count, HD)
    row_delta = jnp.sum(grad_attn_heads.astype(jnp.float32) * attended.astype(jnp.float32), axis=-1)
    prob_rows = jnp.exp(scores - log_total[..., None])
    grad_probs = jnp.einsum(
        "ilhd,imhd->ihlm", grad_attn_heads, value_heads, preferred_element_type=jnp.float32
    )
    grad_scores = (
        prob_rows * (grad_probs - jnp.transpose(row_delta, (0, 2, 1))[..., None]) * score_scale
    ).astype(jnp.bfloat16)
    grad_query = jnp.einsum(
        "ihlm,imhd->ilhd", grad_scores, key_heads, preferred_element_type=jnp.float32
    ).astype(jnp.bfloat16)
    key_terms = jnp.einsum(
        "ihlm,ilhd->imhd", grad_scores, query_heads, preferred_element_type=jnp.float32
    ).astype(jnp.bfloat16)
    value_terms = jnp.einsum(
        "ihlm,ilhd->imhd",
        prob_rows.astype(jnp.bfloat16),
        grad_attn_heads,
        preferred_element_type=jnp.float32,
    ).astype(jnp.bfloat16)
    terms = jnp.stack([key_terms, value_terms]).reshape(
        2, images, seq_size, block_rows, head_cols
    )
    terms = lax.all_to_all(jnp.transpose(terms, (2, 0, 1, 3, 4)), "seq", 0, 0)
    grad_kv = jnp.sum(terms.astype(jnp.float32), axis=0).astype(jnp.bfloat16)
    grad_qkv = jnp.concatenate(
        [grad_query.reshape(1, total_rows, head_cols), grad_kv.reshape(2, total_rows, head_cols)]
    )
    grad_norm_one = scatter_rows(
        jnp.einsum("ktf,kdf->td", grad_qkv, qkv_weight, preferred_element_type=jnp.float32)
    )
    grad_input = (
        grad_resid.astype(jnp.float32) + norm_backward(normed_one, inv_one, grad_norm_one)
    ).astype(jnp.bfloat16)
    return (block_out[None], grad_input[None])


def solution(mesh):
    in_specs = (
        P("section", ("seq", "mp"), None),
        P(None, None, ("section", "mp")),
        P(("section", "mp"), None),
        P(None, ("section", "mp")),
        P(("section", "mp"), None),
        P("section", ("seq", "mp"), None),
    )
    out_specs = (P("section", ("seq", "mp"), None), P("section", ("seq", "mp"), None))
    return jax.shard_map(
        per_device, mesh=mesh, in_specs=in_specs, out_specs=out_specs, check_vma=False
    )
```

```python
import math

import jax
import jax.numpy as jnp
from jax import lax
from jax.experimental import pallas as pl
from jax.experimental.pallas import tpu as pltpu
from jax.sharding import PartitionSpec as P

HD = 128
norm_eps = 1e-06
F32 = jnp.float32
BF16 = jnp.bfloat16
NT = (((1,), (1,)), ((), ()))
NN = (((1,), (0,)), ((), ()))
TN = (((0,), (0,)), ((), ()))


def dot(lhs, rhs, dims=NN):
    return lax.dot_general(lhs, rhs, dims, preferred_element_type=F32)


def whole(shape):
    rank = len(shape)
    return pl.BlockSpec(shape, lambda *ids: (0,) * rank)


def kernel_call(body, name, grid, ins, outs, scratch=(), after=(), flops=0, nbytes=0):
    count = len(ins)

    def run(*refs):
        body(*refs[:count], *refs[count + len(after) :])

    in_specs = [whole(arr.shape) if spec is None else spec for arr, spec in ins]
    in_specs += [pl.BlockSpec(memory_space=pl.ANY)] * len(after)
    out_specs = [whole(shape) if spec is None else spec for shape, _, spec in outs]
    return pl.pallas_call(
        run,
        name=name,
        grid=grid,
        in_specs=in_specs,
        out_specs=out_specs,
        out_shape=[jax.ShapeDtypeStruct(shape, dtype) for shape, dtype, _ in outs],
        scratch_shapes=list(scratch),
        compiler_params=pltpu.CompilerParams(vmem_limit_bytes=16 * 1024 * 1024),
        cost_estimate=pl.CostEstimate(flops=flops, bytes_accessed=nbytes, transcendentals=0),
    )(*[arr for arr, _ in ins], *after)


def hbm(array):
    return pltpu.with_memory_space_constraint(array, pltpu.HBM)


def fetch_body(src_ref, after_ref, dst_ref):
    pltpu.sync_copy(src_ref, dst_ref)


def fetch(weight, after, name):
    return pl.pallas_call(
        fetch_body,
        name=name,
        in_specs=[pl.BlockSpec(memory_space=pltpu.HBM), pl.BlockSpec(memory_space=pl.ANY)],
        out_specs=pl.BlockSpec(memory_space=pltpu.VMEM),
        out_shape=pltpu.VMEM(weight.shape, weight.dtype),
        compiler_params=pltpu.CompilerParams(vmem_limit_bytes=1024 * 1024),
        cost_estimate=pl.CostEstimate(flops=0, bytes_accessed=2 * weight.size, transcendentals=0),
    )(hbm(weight), after)


def local_call(body, name, ins, outs, scratch=(), after=(), flops=0, nbytes=0):
    vmem = pl.BlockSpec(memory_space=pltpu.VMEM)
    count = len(ins)

    def run(*refs):
        body(*refs[:count], *refs[count + len(after) :])

    return pl.pallas_call(
        run,
        name=name,
        in_specs=[vmem] * count + [pl.BlockSpec(memory_space=pl.ANY)] * len(after),
        out_specs=[vmem] * len(outs),
        out_shape=[jax.ShapeDtypeStruct(shape, dtype) for shape, dtype in outs],
        scratch_shapes=list(scratch),
        compiler_params=pltpu.CompilerParams(vmem_limit_bytes=16 * 1024 * 1024),
        cost_estimate=pl.CostEstimate(flops=flops, bytes_accessed=nbytes, transcendentals=0),
    )(*ins, *after)


def row_norm(rows):
    mean = jnp.mean(rows, axis=-1, keepdims=True)
    centered = rows - mean
    inv_std = lax.rsqrt(jnp.mean(centered * centered, axis=-1, keepdims=True) + norm_eps)
    return centered * inv_std, inv_std


def row_norm_backward(normed, inv_std, grad):
    mean_grad = jnp.mean(grad, axis=-1, keepdims=True)
    mean_mix = jnp.mean(grad * normed, axis=-1, keepdims=True)
    return inv_std * (grad - mean_grad - normed * mean_mix)


def add_parts(parts_ref):
    total = parts_ref[0].astype(F32)
    for index in range(1, parts_ref.shape[0]):
        total = total + parts_ref[index].astype(F32)
    return total


def fill_copies(copies_ref, rows):
    for index in range(copies_ref.shape[0]):
        copies_ref[index] = rows


def first_norm_body(in_ref, copies_ref):
    normed, _ = row_norm(in_ref[...].astype(F32))
    fill_copies(copies_ref, normed.astype(BF16))


def second_norm_body(parts_ref, in_ref, resid_ref, copies_ref):
    resid = (in_ref[...].astype(F32) + add_parts(parts_ref)).astype(BF16)
    resid_ref[...] = resid
    normed, _ = row_norm(resid.astype(F32))
    fill_copies(copies_ref, normed.astype(BF16))


def resid_grad_body(parts_ref, resid_ref, cot_ref, grad_ref, copies_ref, mark_ref):
    mark_ref[...] = jnp.zeros_like(mark_ref)
    normed, inv_std = row_norm(resid_ref[...].astype(F32))
    grad = row_norm_backward(normed, inv_std, add_parts(parts_ref))
    grad = (cot_ref[...].astype(F32) + grad).astype(BF16)
    grad_ref[...] = grad
    fill_copies(copies_ref, grad)


def input_grad_body(parts_ref, in_ref, grad_ref, resid_ref, ffn_ref, out_ref, block_ref):
    block_ref[...] = (resid_ref[...].astype(F32) + ffn_ref[...].astype(F32)).astype(BF16)
    normed, inv_std = row_norm(in_ref[...].astype(F32))
    grad = row_norm_backward(normed, inv_std, add_parts(parts_ref))
    out_ref[...] = (grad_ref[...].astype(F32) + grad).astype(BF16)


def pack_place(slot, half_rows):
    image, head, half = slot // 4, (slot // 2) % 2, slot % 2
    row = image * 2 * half_rows
    return row, row + half * half_rows, head * HD


def join_halves(mine_ref, other_ref, rows_ref):
    half = mine_ref.shape[0]
    rows_ref[:half] = mine_ref[...]
    rows_ref[half:] = other_ref[...]


def qkv_body(mine_ref, other_ref, w_ref, pack_ref, rows_ref):
    join_halves(mine_ref, other_ref, rows_ref)
    half_rows = pack_ref.shape[1] // 5
    for part in range(3):
        acc = dot(rows_ref[...], w_ref[part]).astype(BF16)
        for slot in range(8):
            image_row, row, col = pack_place(slot, half_rows)
            if part == 0:
                pack_ref[slot, :half_rows] = acc[row : row + half_rows, col : col + HD]
            else:
                start = half_rows * (2 * part - 1)
                pack_ref[slot, start : start + 2 * half_rows] = acc[
                    image_row : image_row + 2 * half_rows, col : col + HD
                ]


def attention_body(pack_ref, att_ref, lse_ref):
    half_rows = att_ref.shape[1]
    keys = pack_ref[:, half_rows : 3 * half_rows, :].reshape(-1, HD)
    values = pack_ref[:, 3 * half_rows :, :].reshape(-1, HD)
    scale = 1.0 / math.sqrt(HD)
    for chunk in range(4):
        queries = pack_ref[2 * chunk : 2 * chunk + 2, :half_rows, :].reshape(-1, HD)
        scores = dot(keys, queries, NT) * scale
        row_max = jnp.max(scores, axis=0, keepdims=True)
        weights = jnp.exp(scores - row_max)
        total = jnp.sum(weights, axis=0, keepdims=True)
        lse_ref[chunk] = row_max + jnp.log(total)
        mixed = dot(values, weights.astype(BF16), TN) / total
        att_ref[2 * chunk : 2 * chunk + 2] = mixed.T.astype(BF16).reshape(2, half_rows, HD)


def attention_grad_body(pack_ref, att_ref, lse_ref, grad_ref, out_ref):
    half_rows = att_ref.shape[1]
    scale = 1.0 / math.sqrt(HD)
    queries = pack_ref[:, :half_rows, :].reshape(-1, HD)
    grads = grad_ref[...].reshape(-1, HD)
    mix = grads.astype(F32) * att_ref[...].reshape(-1, HD).astype(F32)
    delta = jnp.sum(mix.T, axis=0, keepdims=True)
    lse = jnp.concatenate([lse_ref[chunk] for chunk in range(4)], axis=1)
    query_total = None
    for slot in range(8):
        keys = pack_ref[slot, half_rows : 3 * half_rows, :]
        values = pack_ref[slot, 3 * half_rows :, :]
        probs = jnp.exp(dot(keys, queries, NT) * scale - lse)
        grad_probs = dot(values, grads, NT)
        grad_scores = (probs * (grad_probs - delta) * scale).astype(BF16)
        out_ref[slot, half_rows : 3 * half_rows] = dot(grad_scores, queries).astype(BF16)
        out_ref[slot, 3 * half_rows :] = dot(probs.astype(BF16), grads).astype(BF16)
        term = dot(keys, grad_scores, TN)
        query_total = term if query_total is None else query_total + term
    out_ref[:, :half_rows] = query_total.T.astype(BF16).reshape(8, half_rows, HD)


def put_halves(own_ref, other_ref, cols, total):
    half = own_ref.shape[0]
    own_ref[:, cols] = total[:half]
    other_ref[:, cols] = total[half:].astype(BF16)


def blocks(count, size):
    def run(body):
        @pl.loop(0, count)
        def _(index):
            body(pl.ds(pl.multiple_of(index * size, size), size))

    return run


def out_body(att_ref, w_ref, own_ref, other_ref, rows_ref):
    half_rows = att_ref.shape[1]
    for slot in range(8):
        _, row, col = pack_place(slot, half_rows)
        rows_ref[row : row + half_rows, col : col + HD] = att_ref[slot]

    @blocks(w_ref.shape[1] // 512, 512)
    def _(cols):
        put_halves(own_ref, other_ref, cols, dot(rows_ref[...], w_ref[:, cols]))


def grad_act_body(all_ref, w_ref, out_ref, rows_ref):
    half = all_ref.shape[0] // 2
    section = lax.axis_index("section")

    @pl.when(pl.program_id(0) == 0)
    def _():
        rows_ref[:half] = all_ref[pl.ds(section * half, half)]
        rows_ref[half:] = all_ref[pl.ds((1 - section) * half, half)]

    out_ref[...] = dot(rows_ref[...], w_ref[...], NT)


def hidden_body(mine_ref, other_ref, w_ref, act_ref, hidden_ref, grad_ref, rows_ref):
    join_halves(mine_ref, other_ref, rows_ref)

    @blocks(w_ref.shape[1] // 256, 256)
    def _(cols):
        pre = dot(rows_ref[...], w_ref[:, cols])
        cumul = 0.5 * (1.0 + lax.erf(pre * 0.7071067811865476))
        hidden_ref[:, cols] = (pre * cumul).astype(BF16)
        slope = cumul + pre * jnp.exp(-0.5 * pre * pre) * 0.3989422804014327
        grad_ref[:, cols] = (act_ref[:, cols] * slope).astype(BF16)


def grad_norm_body(rows_ref, w_ref, own_ref, other_ref):
    @blocks(w_ref.shape[0] // 512, 512)
    def _(cols):
        put_halves(own_ref, other_ref, cols, dot(rows_ref[...], w_ref[cols, :], NT))


def down_body(rows_ref, w_ref, own_ref, other_ref):
    put_halves(own_ref, other_ref, slice(None), dot(rows_ref[...], w_ref[...]))


def out_grad_body(mine_ref, other_ref, w_ref, pack_ref):
    half_rows = pack_ref.shape[1]
    for image, rows_ref in enumerate((mine_ref, other_ref)):
        grad = dot(rows_ref[...], w_ref[...], NT).astype(BF16)
        for slot in range(4):
            _, row, col = pack_place(slot, half_rows)
            pack_ref[4 * image + slot] = grad[row : row + half_rows, col : col + HD]


def qkv_grad_body(pack_ref, w_ref, own_ref, other_ref, rows_ref):
    half_rows = pack_ref.shape[1] // 5

    @pl.when(pl.program_id(0) == 0)
    def _():
        for slot in range(8):
            _, row, col = pack_place(slot, half_rows)
            rows_ref[0, row : row + half_rows, col : col + HD] = pack_ref[slot, :half_rows]
        for slot in range(0, 8, 2):
            row, _, col = pack_place(slot, half_rows)
            for part in (1, 2):
                start = half_rows * (2 * part - 1)
                both = pack_ref[slot, start : start + 2 * half_rows].astype(F32) + pack_ref[
                    slot + 1, start : start + 2 * half_rows
                ].astype(F32)
                rows_ref[part, row : row + 2 * half_rows, col : col + HD] = both.astype(BF16)

    total = dot(rows_ref[0], w_ref[0], NT)
    for part in (1, 2):
        total = total + dot(rows_ref[part], w_ref[part], NT)
    put_halves(own_ref, other_ref, slice(None), total)


def swap_section(data):
    return lax.ppermute(data, "section", [(0, 1), (1, 0)])


def exchange(data, axis):
    return lax.all_to_all(data, axis, 0, 0)


def pair_sum(own, other):
    return (own + swap_section(other).astype(F32)).astype(BF16)


def high_groups():
    size = lax.axis_size("mp")
    return [[i, i + size // 2] for i in range(size // 2)]


def low_groups():
    size = lax.axis_size("mp")
    return [list(range(size // 2)), list(range(size // 2, size))]


def per_device(bottleneck, qkv_weight, out_weight, up_weight, down_weight, cotangent):
    own_in = bottleneck[0]
    own_cot = cotangent[0]
    rows, width = own_in.shape
    group = lax.axis_size("mp")
    seq_size = lax.axis_size("seq")
    half = rows * group
    total_rows = 2 * half
    half_rows = half // 2
    head_cols = qkv_weight.shape[2]
    units = up_weight.shape[1]
    assert (total_rows // half) * (head_cols // HD) * 2 == seq_size == 8
    copies = ((group, rows, width), BF16)
    row_out = ((rows, width), BF16)
    halves = [((half, width), F32), ((half, width), BF16)]
    att_shape = ((seq_size, half_rows, HD), BF16)
    pack_shape = ((seq_size, 5 * half_rows, HD), BF16)
    big = 2 * total_rows * width * units
    joined = pltpu.VMEM((total_rows, width), BF16)

    cot_all = lax.all_gather(own_cot, ("section", "mp"), axis=0, tiled=True)

    (send,) = local_call(first_norm_body, "first_norm", [own_in], [copies])
    weight = fetch(qkv_weight, send, "fetch_qkv")
    mine = exchange(send, "mp").reshape(half, width)
    (send,) = local_call(
        qkv_body,
        "qkv",
        [mine, swap_section(mine), weight],
        [pack_shape],
        [joined],
        flops=2 * total_rows * width * 3 * head_cols,
    )
    pack = exchange(send, "seq")
    att, lse = local_call(
        attention_body,
        "attention",
        [pack],
        [att_shape, ((4, 1, 2 * half_rows), F32)],
        flops=4 * half * half * 8 * HD,
    )
    weight = fetch(out_weight, att, "fetch_out")
    got = exchange(att, "seq")
    own, other = local_call(
        out_body,
        "attn_out",
        [got, weight],
        halves,
        [pltpu.VMEM((total_rows, head_cols), BF16)],
        after=[hbm(cot_all)],
        flops=2 * total_rows * width * head_cols,
    )
    send = pair_sum(own, other).reshape(group, rows, width)
    unit_block = units // 4
    unit_spec = pl.BlockSpec((total_rows, unit_block), lambda j: (0, j))
    (grad_act,) = kernel_call(
        grad_act_body,
        "grad_act",
        (4,),
        [
            (hbm(cot_all), None),
            (hbm(down_weight), pl.BlockSpec((unit_block, width), lambda j: (j, 0))),
        ],
        [((total_rows, units), F32, unit_spec)],
        [joined],
        after=[send],
        flops=big,
        nbytes=2 * width * units,
    )
    parts = exchange(send, "mp")
    resid, send = local_call(
        second_norm_body, "second_norm", [parts, own_in], [row_out, copies], after=[grad_act]
    )
    weight = fetch(up_weight, send, "fetch_up")
    mine = exchange(send, "mp").reshape(half, width)
    hidden, grad_hidden = local_call(
        hidden_body,
        "hidden",
        [mine, swap_section(mine), weight, grad_act],
        [((total_rows, units), BF16)] * 2,
        [joined],
        flops=big,
    )
    own, other = local_call(
        grad_norm_body, "grad_norm_two", [grad_hidden, weight], halves, flops=big
    )
    send = pair_sum(own, other).reshape(group, rows, width)
    block = width // 8
    block_spec = pl.BlockSpec((half, block), lambda j: (0, j))
    own, other = kernel_call(
        down_body,
        "down",
        (8,),
        [(hidden, None), (hbm(down_weight), pl.BlockSpec((units, block), lambda j: (0, j)))],
        [(shape, dtype, block_spec) for shape, dtype in halves],
        after=[send],
        flops=big,
        nbytes=2 * width * units,
    )
    parts = exchange(send, "mp")
    grad_resid, send, mark = local_call(
        resid_grad_body,
        "resid_grad",
        [parts, resid, own_cot],
        [row_out, copies, ((8, 128), F32)],
        after=[own],
    )
    weight = fetch(out_weight, send, "fetch_out_again")
    other, mark = lax.optimization_barrier((other, mark))
    mine = exchange(send, "mp").reshape(half, width)
    pair = pair_sum(own, other)
    ffn_high = lax.psum_scatter(
        pair, "mp", scatter_dimension=0, axis_index_groups=high_groups(), tiled=True
    )
    ffn_own = lax.psum_scatter(
        ffn_high, "mp", scatter_dimension=0, axis_index_groups=low_groups(), tiled=True
    )
    (send,) = local_call(
        out_grad_body,
        "attn_out_grad",
        [mine, swap_section(mine), weight],
        [att_shape],
        after=[mark],
        flops=2 * total_rows * width * head_cols,
    )
    grad_att = exchange(send, "seq")
    (send,) = local_call(
        attention_grad_body,
        "attention_grad",
        [pack, att, lse, grad_att],
        [pack_shape],
        after=[ffn_high],
        flops=10 * half * half * 8 * HD,
    )
    got = exchange(send, "seq")
    own, other = kernel_call(
        qkv_grad_body,
        "qkv_grad",
        (8,),
        [
            (got, None),
            (hbm(qkv_weight), pl.BlockSpec((3, block, head_cols), lambda j: (0, j, 0))),
        ],
        [(shape, dtype, block_spec) for shape, dtype in halves],
        [pltpu.VMEM((3, total_rows, head_cols), BF16)],
        flops=2 * total_rows * width * 3 * head_cols,
        nbytes=2 * width * 3 * head_cols,
    )
    parts = exchange(pair_sum(own, other).reshape(group, rows, width), "mp")
    grad_input, block_out = local_call(
        input_grad_body,
        "input_grad",
        [parts, own_in, grad_resid, resid, ffn_own],
        [row_out, row_out],
    )
    return (block_out[None], grad_input[None])


def solution(mesh):
    in_specs = (
        P("section", ("seq", "mp"), None),
        P(None, None, ("section", "mp")),
        P(("section", "mp"), None),
        P(None, ("section", "mp")),
        P(("section", "mp"), None),
        P("section", ("seq", "mp"), None),
    )
    out_specs = (P("section", ("seq", "mp"), None), P("section", ("seq", "mp"), None))
    return jax.shard_map(
        per_device, mesh=mesh, in_specs=in_specs, out_specs=out_specs, check_vma=False
    )
```

```python
import functools
import math

import jax
import jax.numpy as jnp
from jax import lax
from jax.experimental import pallas as pl
from jax.experimental.pallas import tpu as pltpu
from jax.sharding import PartitionSpec as P

HD = 128
norm_eps = 1e-06
F32 = jnp.float32
BF16 = jnp.bfloat16
NT = (((1,), (1,)), ((), ()))
NN = (((1,), (0,)), ((), ()))
TN = (((0,), (0,)), ((), ()))


def dot(lhs, rhs, dims=NN):
    return lax.dot_general(lhs, rhs, dims, preferred_element_type=F32)


def whole(shape):
    rank = len(shape)
    return pl.BlockSpec(shape, lambda *ids: (0,) * rank)


def kernel_call(body, name, grid, ins, outs, scratch=(), after=(), flops=0, nbytes=0):
    count = len(ins)

    def run(*refs):
        body(*refs[:count], *refs[count + len(after) :])

    in_specs = [whole(arr.shape) if spec is None else spec for arr, spec in ins]
    in_specs += [pl.BlockSpec(memory_space=pl.ANY)] * len(after)
    out_specs = [whole(shape) if spec is None else spec for shape, _, spec in outs]
    return pl.pallas_call(
        run,
        name=name,
        grid=grid,
        in_specs=in_specs,
        out_specs=out_specs,
        out_shape=[jax.ShapeDtypeStruct(shape, dtype) for shape, dtype, _ in outs],
        scratch_shapes=list(scratch),
        compiler_params=pltpu.CompilerParams(vmem_limit_bytes=16 * 1024 * 1024),
        cost_estimate=pl.CostEstimate(flops=flops, bytes_accessed=nbytes, transcendentals=0),
    )(*[arr for arr, _ in ins], *after)


def hbm(array):
    return pltpu.with_memory_space_constraint(array, pltpu.HBM)


def fetch(weight, after, name, part=0, parts=1):
    rows = weight.shape[0] // parts

    def fetch_body(src_ref, after_ref, dst_ref):
        pltpu.sync_copy(src_ref.at[pl.ds(part * rows, rows)], dst_ref)

    return pl.pallas_call(
        fetch_body,
        name=name,
        in_specs=[pl.BlockSpec(memory_space=pltpu.HBM), pl.BlockSpec(memory_space=pl.ANY)],
        out_specs=pl.BlockSpec(memory_space=pltpu.VMEM),
        out_shape=pltpu.VMEM((rows,) + weight.shape[1:], weight.dtype),
        compiler_params=pltpu.CompilerParams(vmem_limit_bytes=1024 * 1024),
        cost_estimate=pl.CostEstimate(
            flops=0, bytes_accessed=2 * weight.size // parts, transcendentals=0
        ),
    )(hbm(weight), after)


def local_call(
    body, name, ins, outs, scratch=(), after=(), late=(), aliases=None, flops=0, nbytes=0
):
    vmem = pl.BlockSpec(memory_space=pltpu.VMEM)
    count, extra = len(ins), len(late)

    def run(*refs):
        sources = refs[count : count + extra]
        rest = refs[count + extra + len(after) :]
        if not extra:
            body(*refs[:count], *rest)
            return
        buffers, sems = rest[-1 - extra : -1], rest[-1]
        moves = [
            pltpu.make_async_copy(source, buffer, sems.at[index])
            for index, (source, buffer) in enumerate(zip(sources, buffers))
        ]
        for move in moves:
            move.start()

        def wait():
            for move in moves:
                move.wait()

        body(*refs[:count], *buffers, *rest[: -1 - extra], wait)

    scratch = list(scratch)
    if extra:
        scratch += [pltpu.VMEM(arr.shape, arr.dtype) for arr in late]
        scratch.append(pltpu.SemaphoreType.DMA((extra,)))
    return pl.pallas_call(
        run,
        name=name,
        in_specs=[vmem] * count + [pl.BlockSpec(memory_space=pl.ANY)] * (extra + len(after)),
        out_specs=[vmem] * len(outs),
        out_shape=[jax.ShapeDtypeStruct(shape, dtype) for shape, dtype in outs],
        scratch_shapes=scratch,
        input_output_aliases=aliases or {},
        compiler_params=pltpu.CompilerParams(vmem_limit_bytes=16 * 1024 * 1024),
        cost_estimate=pl.CostEstimate(flops=flops, bytes_accessed=nbytes, transcendentals=0),
    )(*ins, *late, *after)


def row_norm(rows):
    mean = jnp.mean(rows, axis=-1, keepdims=True)
    centered = rows - mean
    inv_std = lax.rsqrt(jnp.mean(centered * centered, axis=-1, keepdims=True) + norm_eps)
    return centered * inv_std, inv_std


def row_norm_backward(normed, inv_std, grad):
    mean_grad = jnp.mean(grad, axis=-1, keepdims=True)
    mean_mix = jnp.mean(grad * normed, axis=-1, keepdims=True)
    return inv_std * (grad - mean_grad - normed * mean_mix)


def add_parts(parts_ref):
    total = parts_ref[0].astype(F32)
    for index in range(1, parts_ref.shape[0]):
        total = total + parts_ref[index].astype(F32)
    return total


def fill_copies(copies_ref, rows):
    for index in range(copies_ref.shape[0]):
        copies_ref[index] = rows


def first_norm_body(in_ref, copies_ref):
    normed, _ = row_norm(in_ref[...].astype(F32))
    fill_copies(copies_ref, normed.astype(BF16))


def second_norm_body(parts_ref, in_ref, resid_ref, copies_ref):
    total = add_parts(parts_ref)
    resid = (in_ref[...].astype(F32) + total).astype(BF16)
    resid_ref[...] = resid
    normed, _ = row_norm(resid.astype(F32))
    fill_copies(copies_ref, normed.astype(BF16))


def resid_grad_body(parts_ref, resid_ref, cot_ref, grad_ref, copies_ref, mark_ref):
    mark_ref[...] = jnp.zeros_like(mark_ref)
    total = add_parts(parts_ref)
    normed, inv_std = row_norm(resid_ref[...].astype(F32))
    grad = row_norm_backward(normed, inv_std, total)
    grad = (cot_ref[...].astype(F32) + grad).astype(BF16)
    grad_ref[...] = grad
    fill_copies(copies_ref, grad)


def input_grad_body(
    parts_ref, in_ref, grad_ref, resid_ref, near_ref, far_ref, out_ref, block_ref, wait
):
    total = add_parts(parts_ref)
    wait()
    ffn = near_ref[...].astype(F32) + far_ref[...].astype(F32)
    block_ref[...] = (resid_ref[...].astype(F32) + ffn).astype(BF16)
    normed, inv_std = row_norm(in_ref[...].astype(F32))
    grad = row_norm_backward(normed, inv_std, total)
    out_ref[...] = (grad_ref[...].astype(F32) + grad).astype(BF16)


def pack_place(slot, half_rows):
    image, head, half = slot // 4, (slot // 2) % 2, slot % 2
    row = image * 2 * half_rows
    return row, row + half * half_rows, head * HD


def join_halves(mine_ref, other_ref, rows_ref):
    half = mine_ref.shape[0]
    rows_ref[:half] = mine_ref[...]
    rows_ref[half:] = other_ref[...]


def qkv_body(
    mine_ref, other_ref, w_ref, pack_ref, rows_ref
):
    join_halves(mine_ref, other_ref, rows_ref)
    half_rows = pack_ref.shape[1] // 5
    for part in range(3):
        acc = dot(rows_ref[...], w_ref[part]).astype(BF16)
        for slot in range(8):
            image_row, row, col = pack_place(slot, half_rows)
            if part == 0:
                pack_ref[slot, :half_rows] = acc[row : row + half_rows, col : col + HD]
            else:
                start = half_rows * (2 * part - 1)
                pack_ref[slot, start : start + 2 * half_rows] = acc[
                    image_row : image_row + 2 * half_rows, col : col + HD
                ]


def attention_body(pack_ref, att_ref, lse_ref):
    half_rows = att_ref.shape[1]
    keys = pack_ref[:, half_rows : 3 * half_rows, :].reshape(-1, HD)
    values = pack_ref[:, 3 * half_rows :, :].reshape(-1, HD)
    scale = 1.0 / math.sqrt(HD)
    for chunk in range(4):
        queries = pack_ref[2 * chunk : 2 * chunk + 2, :half_rows, :].reshape(-1, HD)
        scores = dot(keys, queries, NT) * scale
        row_max = jnp.max(scores, axis=0, keepdims=True)
        weights = jnp.exp(scores - row_max)
        total = jnp.sum(weights, axis=0, keepdims=True)
        lse_ref[chunk] = row_max + jnp.log(total)
        mixed = dot(values, weights.astype(BF16), TN) / total
        att_ref[2 * chunk : 2 * chunk + 2] = mixed.T.astype(BF16).reshape(2, half_rows, HD)


def attention_grad_body(pack_ref, att_ref, lse_ref, grad_ref, out_ref):
    half_rows = att_ref.shape[1]
    scale = 1.0 / math.sqrt(HD)
    queries = pack_ref[:, :half_rows, :].reshape(-1, HD)
    grads = grad_ref[...].reshape(-1, HD)
    mix = grads.astype(F32) * att_ref[...].reshape(-1, HD).astype(F32)
    delta = jnp.sum(mix.T, axis=0, keepdims=True)
    lse = jnp.concatenate([lse_ref[chunk] for chunk in range(4)], axis=1)
    query_total = None
    for slot in range(8):
        keys = pack_ref[slot, half_rows : 3 * half_rows, :]
        values = pack_ref[slot, 3 * half_rows :, :]
        probs = jnp.exp(dot(keys, queries, NT) * scale - lse)
        grad_probs = dot(values, grads, NT)
        grad_scores = (probs * (grad_probs - delta) * scale).astype(BF16)
        out_ref[slot, half_rows : 3 * half_rows] = dot(grad_scores, queries).astype(BF16)
        out_ref[slot, 3 * half_rows :] = dot(probs.astype(BF16), grads).astype(BF16)
        term = dot(keys, grad_scores, TN)
        query_total = term if query_total is None else query_total + term
    out_ref[:, :half_rows] = query_total.T.astype(BF16).reshape(8, half_rows, HD)


def put_halves(own_ref, other_ref, cols, total):
    half = own_ref.shape[0]
    own_ref[:, cols] = total[:half].astype(BF16)
    other_ref[:, cols] = total[half:].astype(BF16)


def out_body(start, att_ref, w_ref, own_ref, other_ref, rows_ref):
    half_rows = att_ref.shape[1]
    for slot in range(8):
        _, row, col = pack_place(slot, half_rows)
        rows_ref[row : row + half_rows, col : col + HD] = att_ref[slot]
    size = 512
    for step in range(own_ref.shape[1] // size):
        cols = slice(start + step * size, start + (step + 1) * size)
        total = dot(rows_ref[...], w_ref[:, cols])
        put_halves(own_ref, other_ref, slice(step * size, (step + 1) * size), total)


def join_low_body(*refs):
    out_ref = refs[-1]
    count = len(refs) - 1
    low = lax.rem(lax.axis_index("mp"), count)
    high = lax.axis_index("mp") // count
    rows = refs[0].shape[1]
    for step in range(count):
        source = lax.rem(low + count - step, count)
        for side, place in ((0, high), (1, 1 - high)):
            start = pl.multiple_of((place * count + source) * rows, rows)
            out_ref[pl.ds(start, rows)] = refs[step][side]


def split_low_body(own_ref, other_ref, *out_refs):
    count = len(out_refs)
    low = lax.rem(lax.axis_index("mp"), count)
    high = lax.axis_index("mp") // count
    rows = out_refs[0].shape[1]
    for step in range(count):
        target = lax.rem(low + step, count)
        for side, place in ((0, high), (1, 1 - high)):
            start = pl.multiple_of((place * count + target) * rows, rows)
            total = own_ref[pl.ds(start, rows)].astype(F32) + other_ref[pl.ds(start, rows)].astype(F32)
            out_refs[step][side] = total.astype(BF16)


def sum_low_body(*refs):
    near_ref, far_ref = refs[-2:]
    for side, out_ref in enumerate((near_ref, far_ref)):
        total = refs[0][side].astype(F32)
        for ref in refs[1:-2]:
            total = total + ref[side].astype(F32)
        out_ref[...] = total.astype(BF16)


def grad_act_body(mine_ref, other_ref, w_ref, out_ref, rows_ref):
    @pl.when(pl.program_id(0) == 0)
    def _():
        join_halves(mine_ref, other_ref, rows_ref)

    out_ref[...] = dot(rows_ref[...], w_ref[...], NT)


def hidden_body(
    mine_ref, other_ref, w_ref, act_ref, hidden_ref, grad_ref, rows_ref
):
    join_halves(mine_ref, other_ref, rows_ref)

    for step in range(w_ref.shape[1] // 256):
        cols = slice(step * 256, (step + 1) * 256)
        pre = dot(rows_ref[...], w_ref[:, cols])
        cumul = 0.5 * (1.0 + lax.erf(pre * 0.7071067811865476))
        hidden_ref[:, cols] = (pre * cumul).astype(BF16)
        slope = cumul + pre * jnp.exp(-0.5 * pre * pre) * 0.3989422804014327
        grad_ref[:, cols] = (act_ref[:, cols] * slope).astype(BF16)


def grad_norm_body(start, rows_ref, w_ref, own_ref, other_ref):
    size = 512
    for step in range(own_ref.shape[1] // size):
        source = slice(start + step * size, start + (step + 1) * size)
        total = dot(rows_ref[...], w_ref[source, :], NT)
        put_halves(own_ref, other_ref, slice(step * size, (step + 1) * size), total)


def pair_body(*refs):
    out_ref = refs[-1]
    size = refs[0].shape[1]
    for index in range(2):
        total = refs[2 * index][...].astype(F32) + refs[2 * index + 1][...].astype(F32)
        out_ref[:, index * size : (index + 1) * size] = total.astype(BF16)


def down_body(rows_ref, w_ref, own_ref, other_ref):
    put_halves(own_ref, other_ref, slice(None), dot(rows_ref[...], w_ref[...]))


def out_grad_body(mine_ref, other_ref, w_ref, pack_ref, rows_ref):
    join_halves(mine_ref, other_ref, rows_ref)
    half_rows = pack_ref.shape[1]
    grad = dot(rows_ref[...], w_ref[...], NT).astype(BF16)
    for slot in range(8):
        _, row, col = pack_place(slot, half_rows)
        pack_ref[slot] = grad[row : row + half_rows, col : col + HD]


def qkv_grad_body(base, pack_ref, w_ref, *refs):
    own_ref, other_ref, rows_ref, w_buf, sems = refs[-5:]
    half_rows = pack_ref.shape[1] // 5
    steps = sems.shape[0]
    size = w_buf.shape[1] // steps

    def move(step):
        source = pl.ds(base + step * size, size)
        cols = pl.ds(step * size, size)
        return pltpu.make_async_copy(w_ref.at[:, source, :], w_buf.at[:, cols, :], sems.at[step])

    for step in range(steps):
        move(step).start()
    for slot in range(8):
        _, row, col = pack_place(slot, half_rows)
        rows_ref[0, row : row + half_rows, col : col + HD] = pack_ref[slot, :half_rows]
    for slot in range(0, 8, 2):
        row, _, col = pack_place(slot, half_rows)
        for part in (1, 2):
            start = half_rows * (2 * part - 1)
            both = pack_ref[slot, start : start + 2 * half_rows].astype(F32) + pack_ref[
                slot + 1, start : start + 2 * half_rows
            ].astype(F32)
            rows_ref[part, row : row + 2 * half_rows, col : col + HD] = both.astype(BF16)

    for step in range(steps):
        move(step).wait()
        cols = slice(step * size, (step + 1) * size)
        total = dot(rows_ref[0], w_buf[0, cols, :], NT)
        for part in (1, 2):
            total = total + dot(rows_ref[part], w_buf[part, cols, :], NT)
        put_halves(own_ref, other_ref, cols, total)


def swap_section(data):
    return lax.ppermute(data, "section", [(0, 1), (1, 0)])


def exchange(data, axis):
    return lax.all_to_all(data, axis, 0, 0)


def by_columns(partial, half, width, after=()):
    sides = [partial(start) for start in (0, width // 2)]
    ins = []
    for own, other in sides:
        ins += [own, swap_section(other)]
    (total,) = local_call(pair_body, "pair", ins, [((half, width), BF16)], after=after)
    return total


def pair_sum(own, other):
    return (own.astype(F32) + swap_section(other).astype(F32)).astype(BF16)


def shift_high(data):
    size = lax.axis_size("mp")
    return lax.ppermute(data, "mp", [(i, (i + size // 2) % size) for i in range(size)])


def shift_low(data, step):
    size = lax.axis_size("mp") // 2
    pairs = [(h * size + i, h * size + (i + step) % size) for h in range(2) for i in range(size)]
    return lax.ppermute(data, "mp", pairs)


def per_device(bottleneck, qkv_weight, out_weight, up_weight, down_weight, cotangent):
    own_in = bottleneck[0]
    own_cot = cotangent[0]
    rows, width = own_in.shape
    group = lax.axis_size("mp")
    seq_size = lax.axis_size("seq")
    half = rows * group
    total_rows = 2 * half
    half_rows = half // 2
    head_cols = qkv_weight.shape[2]
    units = up_weight.shape[1]
    assert (total_rows // half) * (head_cols // HD) * 2 == seq_size == 8
    copies = ((group, rows, width), BF16)
    row_out = ((rows, width), BF16)
    halves = [((half, width), BF16)] * 2
    column_halves = [((half, width // 2), BF16)] * 2
    att_shape = ((seq_size, half_rows, HD), BF16)
    pack_shape = ((seq_size, 5 * half_rows, HD), BF16)
    big = 2 * total_rows * width * units
    joined = pltpu.VMEM((total_rows, width), BF16)

    (send,) = local_call(first_norm_body, "first_norm", [own_in], [copies])
    send, cot_near = lax.optimization_barrier((send, own_cot))
    cot_far = shift_high(cot_near)
    weight = fetch(qkv_weight, send, "fetch_qkv")
    mine, cot_far = lax.optimization_barrier((exchange(send, "mp"), cot_far))
    mine = mine.reshape(half, width)
    cot_two = jnp.stack([cot_near, cot_far])
    (send,) = local_call(
        qkv_body,
        "qkv",
        [mine, swap_section(mine), weight],
        [pack_shape],
        [joined],
        flops=2 * total_rows * width * 3 * head_cols,
    )
    send, cot_two = lax.optimization_barrier((send, cot_two))
    pack = exchange(send, "seq")
    cot_shifted = [shift_low(cot_two, step) for step in range(1, group // 2)]
    att, lse = local_call(
        attention_body,
        "attention",
        [pack],
        [att_shape, ((4, 1, 2 * half_rows), F32)],
        flops=4 * half * half * 8 * HD,
    )
    weight = fetch(out_weight, att, "fetch_out")
    got = exchange(att, "seq")
    (cot_mine,) = local_call(
        join_low_body,
        "join_cotangent",
        [cot_two, *cot_shifted],
        [((half, width), BF16)],
        after=[att],
    )
    cots = [cot_mine, swap_section(cot_mine)]

    def attn_out(start):
        return local_call(
            functools.partial(out_body, start),
            "attn_out",
            [got, weight],
            column_halves,
            [pltpu.VMEM((total_rows, head_cols), BF16)],
            after=[cot_mine],
        )

    send = by_columns(attn_out, half, width).reshape(group, rows, width)
    unit_block = units // 4
    unit_spec = pl.BlockSpec((total_rows, unit_block), lambda j: (0, j))
    (grad_act,) = kernel_call(
        grad_act_body,
        "grad_act",
        (4,),
        [
            *[(cot, None) for cot in cots],
            (hbm(down_weight), pl.BlockSpec((unit_block, width), lambda j: (j, 0))),
        ],
        [((total_rows, units), F32, unit_spec)],
        [joined],
        after=[send],
        flops=big,
        nbytes=2 * width * units,
    )
    parts = exchange(send, "mp")
    resid, send = local_call(
        second_norm_body, "second_norm", [parts, own_in], [row_out, copies], after=[grad_act]
    )
    mine = exchange(send, "mp").reshape(half, width)
    weight = fetch(up_weight, send, "fetch_up")
    hidden, grad_hidden = local_call(
        hidden_body,
        "hidden",
        [mine, swap_section(mine), weight, grad_act],
        [((total_rows, units), BF16)] * 2,
        [joined],
        flops=big,
    )

    def grad_norm_two(start):
        return local_call(
            functools.partial(grad_norm_body, start),
            "grad_norm_two",
            [grad_hidden, weight],
            column_halves,
        )

    send = by_columns(grad_norm_two, half, width).reshape(group, rows, width)
    block = width // 8
    block_spec = pl.BlockSpec((half, block), lambda j: (0, j))
    own, other = kernel_call(
        down_body,
        "down",
        (8,),
        [(hidden, None), (hbm(down_weight), pl.BlockSpec((units, block), lambda j: (0, j)))],
        [(shape, dtype, block_spec) for shape, dtype in halves],
        after=[send],
        flops=big,
        nbytes=2 * width * units,
    )
    parts = exchange(send, "mp")
    grad_resid, send, mark = local_call(
        resid_grad_body,
        "resid_grad",
        [parts, resid, own_cot],
        [row_out, copies, ((8, 128), F32)],
        after=[own],
    )
    weight = fetch(out_weight, send, "fetch_out_again")
    other, mark = lax.optimization_barrier((other, mark))
    sums_low = local_call(
        split_low_body,
        "split_sums",
        [own, swap_section(other)],
        [((2, rows, width), BF16)] * (group // 2),
    )
    mine, *sums_low = lax.optimization_barrier((exchange(send, "mp"), *sums_low))
    mine = mine.reshape(half, width)
    (send,) = local_call(
        out_grad_body,
        "attn_out_grad",
        [mine, swap_section(mine), weight],
        [att_shape],
        [joined],
        after=[mark],
        flops=2 * total_rows * width * head_cols,
    )
    grad_att = exchange(send, "seq")
    (send,) = local_call(
        attention_grad_body,
        "attention_grad",
        [pack, att, lse, grad_att],
        [pack_shape],
        flops=10 * half * half * 8 * HD,
    )
    send, *sums_low = lax.optimization_barrier((send, *sums_low))
    shifted = [shift_low(sums_low[step], step) for step in range(1, group // 2)]
    sum_near, sum_far = local_call(
        sum_low_body, "join_sums", [sums_low[0], *shifted], [row_out] * 2
    )
    sum_far = shift_high(sum_far)
    got = exchange(send, "seq")
    vmem = pl.BlockSpec(memory_space=pltpu.VMEM)

    def qkv_grad(start):
        after = shifted if start == 0 else [sum_near]
        return pl.pallas_call(
            functools.partial(qkv_grad_body, start),
            name="qkv_grad",
            in_specs=[vmem, pl.BlockSpec(memory_space=pltpu.HBM)]
            + [pl.BlockSpec(memory_space=pl.ANY)] * len(after),
            out_specs=[vmem] * 2,
            out_shape=[jax.ShapeDtypeStruct(shape, dtype) for shape, dtype in column_halves],
            scratch_shapes=[
                pltpu.VMEM((3, total_rows, head_cols), BF16),
                pltpu.VMEM((3, width // 2, head_cols), BF16),
                pltpu.SemaphoreType.DMA((4,)),
            ],
            compiler_params=pltpu.CompilerParams(vmem_limit_bytes=16 * 1024 * 1024),
            cost_estimate=pl.CostEstimate(flops=0, bytes_accessed=0, transcendentals=0),
        )(got, hbm(qkv_weight), *after)

    parts = exchange(by_columns(qkv_grad, half, width, [sum_far]).reshape(group, rows, width), "mp")
    grad_input, block_out = local_call(
        input_grad_body,
        "input_grad",
        [parts],
        [row_out, row_out],
        late=[hbm(own_in), grad_resid, resid, sum_near, sum_far],
    )
    return (block_out[None], grad_input[None])


def solution(mesh):
    in_specs = (
        P("section", ("seq", "mp"), None),
        P(None, None, ("section", "mp")),
        P(("section", "mp"), None),
        P(None, ("section", "mp")),
        P(("section", "mp"), None),
        P("section", ("seq", "mp"), None),
    )
    out_specs = (P("section", ("seq", "mp"), None), P("section", ("seq", "mp"), None))
    return jax.shard_map(
        per_device, mesh=mesh, in_specs=in_specs, out_specs=out_specs, check_vma=False
    )
```

```python
import functools
import math

import jax
import jax.numpy as jnp
from jax import lax
from jax.experimental import pallas as pl
from jax.experimental.pallas import tpu as pltpu
from jax.sharding import PartitionSpec as P

HD = 128
norm_eps = 1e-06
F32 = jnp.float32
BF16 = jnp.bfloat16
NT = (((1,), (1,)), ((), ()))
NN = (((1,), (0,)), ((), ()))
TN = (((0,), (0,)), ((), ()))


def dot(lhs, rhs, dims=NN):
    return lax.dot_general(lhs, rhs, dims, preferred_element_type=F32)


def whole(shape):
    rank = len(shape)
    return pl.BlockSpec(shape, lambda *ids: (0,) * rank)


def kernel_call(body, name, grid, ins, outs, scratch=(), after=(), flops=0, nbytes=0):
    count = len(ins)

    def run(*refs):
        body(*refs[:count], *refs[count + len(after) :])

    in_specs = [whole(arr.shape) if spec is None else spec for arr, spec in ins]
    in_specs += [pl.BlockSpec(memory_space=pl.ANY)] * len(after)
    out_specs = [whole(shape) if spec is None else spec for shape, _, spec in outs]
    return pl.pallas_call(
        run,
        name=name,
        grid=grid,
        in_specs=in_specs,
        out_specs=out_specs,
        out_shape=[jax.ShapeDtypeStruct(shape, dtype) for shape, dtype, _ in outs],
        scratch_shapes=list(scratch),
        compiler_params=pltpu.CompilerParams(vmem_limit_bytes=16 * 1024 * 1024),
        cost_estimate=pl.CostEstimate(flops=flops, bytes_accessed=nbytes, transcendentals=0),
    )(*[arr for arr, _ in ins], *after)


def hbm(array):
    return pltpu.with_memory_space_constraint(array, pltpu.HBM)


def fetch(weight, after, name, part=0, parts=1):
    rows = weight.shape[0] // parts

    def fetch_body(src_ref, after_ref, dst_ref):
        pltpu.sync_copy(src_ref.at[pl.ds(part * rows, rows)], dst_ref)

    return pl.pallas_call(
        fetch_body,
        name=name,
        in_specs=[pl.BlockSpec(memory_space=pltpu.HBM), pl.BlockSpec(memory_space=pl.ANY)],
        out_specs=pl.BlockSpec(memory_space=pltpu.VMEM),
        out_shape=pltpu.VMEM((rows,) + weight.shape[1:], weight.dtype),
        compiler_params=pltpu.CompilerParams(vmem_limit_bytes=1024 * 1024),
        cost_estimate=pl.CostEstimate(
            flops=0, bytes_accessed=2 * weight.size // parts, transcendentals=0
        ),
    )(hbm(weight), after)


def local_call(
    body, name, ins, outs, scratch=(), after=(), late=(), aliases=None, flops=0, nbytes=0
):
    vmem = pl.BlockSpec(memory_space=pltpu.VMEM)
    count, extra = len(ins), len(late)

    def run(*refs):
        sources = refs[count : count + extra]
        rest = refs[count + extra + len(after) :]
        if not extra:
            body(*refs[:count], *rest)
            return
        buffers, sems = rest[-1 - extra : -1], rest[-1]
        moves = [
            pltpu.make_async_copy(source, buffer, sems.at[index])
            for index, (source, buffer) in enumerate(zip(sources, buffers))
        ]
        for move in moves:
            move.start()

        def wait():
            for move in moves:
                move.wait()

        body(*refs[:count], *buffers, *rest[: -1 - extra], wait)

    scratch = list(scratch)
    if extra:
        scratch += [pltpu.VMEM(arr.shape, arr.dtype) for arr in late]
        scratch.append(pltpu.SemaphoreType.DMA((extra,)))
    return pl.pallas_call(
        run,
        name=name,
        in_specs=[vmem] * count + [pl.BlockSpec(memory_space=pl.ANY)] * (extra + len(after)),
        out_specs=[vmem] * len(outs),
        out_shape=[jax.ShapeDtypeStruct(shape, dtype) for shape, dtype in outs],
        scratch_shapes=scratch,
        input_output_aliases=aliases or {},
        compiler_params=pltpu.CompilerParams(vmem_limit_bytes=16 * 1024 * 1024),
        cost_estimate=pl.CostEstimate(flops=flops, bytes_accessed=nbytes, transcendentals=0),
    )(*ins, *late, *after)


def row_norm(rows):
    mean = jnp.mean(rows, axis=-1, keepdims=True)
    centered = rows - mean
    inv_std = lax.rsqrt(jnp.mean(centered * centered, axis=-1, keepdims=True) + norm_eps)
    return centered * inv_std, inv_std


def row_norm_backward(normed, inv_std, grad):
    mean_grad = jnp.mean(grad, axis=-1, keepdims=True)
    mean_mix = jnp.mean(grad * normed, axis=-1, keepdims=True)
    return inv_std * (grad - mean_grad - normed * mean_mix)


def add_parts(parts_ref):
    total = parts_ref[0].astype(F32)
    for index in range(1, parts_ref.shape[0]):
        total = total + parts_ref[index].astype(F32)
    return total


def fill_copies(copies_ref, rows):
    for index in range(copies_ref.shape[0]):
        copies_ref[index] = rows


def first_norm_body(in_ref, copies_ref):
    normed, _ = row_norm(in_ref[...].astype(F32))
    fill_copies(copies_ref, normed.astype(BF16))


def second_norm_body(parts_ref, in_ref, resid_ref, copies_ref):
    total = add_parts(parts_ref)
    resid = (in_ref[...].astype(F32) + total).astype(BF16)
    resid_ref[...] = resid
    normed, _ = row_norm(resid.astype(F32))
    fill_copies(copies_ref, normed.astype(BF16))


def resid_grad_body(parts_ref, resid_ref, cot_ref, grad_ref, copies_ref, mark_ref):
    mark_ref[...] = jnp.zeros_like(mark_ref)
    total = add_parts(parts_ref)
    normed, inv_std = row_norm(resid_ref[...].astype(F32))
    grad = row_norm_backward(normed, inv_std, total)
    grad = (cot_ref[...].astype(F32) + grad).astype(BF16)
    grad_ref[...] = grad
    fill_copies(copies_ref, grad)


def input_grad_body(
    parts_ref, in_ref, grad_ref, resid_ref, near_ref, far_ref, out_ref, block_ref, wait
):
    total = add_parts(parts_ref)
    wait()
    ffn = near_ref[...].astype(F32) + far_ref[...].astype(F32)
    block_ref[...] = (resid_ref[...].astype(F32) + ffn).astype(BF16)
    normed, inv_std = row_norm(in_ref[...].astype(F32))
    grad = row_norm_backward(normed, inv_std, total)
    out_ref[...] = (grad_ref[...].astype(F32) + grad).astype(BF16)


def pack_place(slot, half_rows):
    image, head, half = slot // 4, (slot // 2) % 2, slot % 2
    row = image * 2 * half_rows
    return row, row + half * half_rows, head * HD


def join_halves(mine_ref, other_ref, rows_ref):
    half = mine_ref.shape[0]
    rows_ref[:half] = mine_ref[...]
    rows_ref[half:] = other_ref[...]


def qkv_body(
    mine_ref, other_ref, w_ref, pack_ref, rows_ref
):
    join_halves(mine_ref, other_ref, rows_ref)
    half_rows = pack_ref.shape[1] // 5
    for part in range(3):
        acc = dot(rows_ref[...], w_ref[part]).astype(BF16)
        for slot in range(8):
            image_row, row, col = pack_place(slot, half_rows)
            if part == 0:
                pack_ref[slot, :half_rows] = acc[row : row + half_rows, col : col + HD]
            else:
                start = half_rows * (2 * part - 1)
                pack_ref[slot, start : start + 2 * half_rows] = acc[
                    image_row : image_row + 2 * half_rows, col : col + HD
                ]


def attention_body(pack_ref, att_ref, lse_ref):
    half_rows = att_ref.shape[1]
    keys = pack_ref[:, half_rows : 3 * half_rows, :].reshape(-1, HD)
    values = pack_ref[:, 3 * half_rows :, :].reshape(-1, HD)
    scale = 1.0 / math.sqrt(HD)
    for chunk in range(4):
        queries = pack_ref[2 * chunk : 2 * chunk + 2, :half_rows, :].reshape(-1, HD)
        scores = dot(keys, queries, NT) * scale
        row_max = jnp.max(scores, axis=0, keepdims=True)
        weights = jnp.exp(scores - row_max)
        total = jnp.sum(weights, axis=0, keepdims=True)
        lse_ref[chunk] = row_max + jnp.log(total)
        mixed = dot(values, weights.astype(BF16), TN) / total
        att_ref[2 * chunk : 2 * chunk + 2] = mixed.T.astype(BF16).reshape(2, half_rows, HD)


def attention_grad_body(pack_ref, att_ref, lse_ref, grad_ref, out_ref):
    half_rows = att_ref.shape[1]
    scale = 1.0 / math.sqrt(HD)
    queries = pack_ref[:, :half_rows, :].reshape(-1, HD)
    grads = grad_ref[...].reshape(-1, HD)
    mix = grads.astype(F32) * att_ref[...].reshape(-1, HD).astype(F32)
    delta = jnp.sum(mix.T, axis=0, keepdims=True)
    lse = jnp.concatenate([lse_ref[chunk] for chunk in range(4)], axis=1)
    query_total = None
    for slot in range(8):
        keys = pack_ref[slot, half_rows : 3 * half_rows, :]
        values = pack_ref[slot, 3 * half_rows :, :]
        probs = jnp.exp(dot(keys, queries, NT) * scale - lse)
        grad_probs = dot(values, grads, NT)
        grad_scores = (probs * (grad_probs - delta) * scale).astype(BF16)
        out_ref[slot, half_rows : 3 * half_rows] = dot(grad_scores, queries).astype(BF16)
        out_ref[slot, 3 * half_rows :] = dot(probs.astype(BF16), grads).astype(BF16)
        term = dot(keys, grad_scores, TN)
        query_total = term if query_total is None else query_total + term
    out_ref[:, :half_rows] = query_total.T.astype(BF16).reshape(8, half_rows, HD)


def put_halves(own_ref, other_ref, cols, total):
    half = own_ref.shape[0]
    own_ref[:, cols] = total[:half].astype(BF16)
    other_ref[:, cols] = total[half:].astype(BF16)


def out_body(start, att_ref, w_ref, own_ref, other_ref, rows_ref):
    half_rows = att_ref.shape[1]
    for slot in range(8):
        _, row, col = pack_place(slot, half_rows)
        rows_ref[row : row + half_rows, col : col + HD] = att_ref[slot]
    size = 512
    for step in range(own_ref.shape[1] // size):
        cols = slice(start + step * size, start + (step + 1) * size)
        total = dot(rows_ref[...], w_ref[:, cols])
        put_halves(own_ref, other_ref, slice(step * size, (step + 1) * size), total)


def join_low_body(*refs):
    *block_refs, _, out_ref, sems = refs
    count = len(block_refs)
    low = lax.rem(lax.axis_index("mp"), count)
    high = lax.axis_index("mp") // count
    rows = block_refs[0].shape[1]
    moves = []
    for step in range(count):
        source = lax.rem(low + count - step, count)
        for side, place in ((0, high), (1, 1 - high)):
            start = pl.multiple_of((place * count + source) * rows, rows)
            moves.append(
                pltpu.make_async_copy(
                    block_refs[step].at[side], out_ref.at[pl.ds(start, rows)], sems.at[step, side]
                )
            )
    for move in moves:
        move.start()
    for move in moves:
        move.wait()


def join_low(blocks, after, shape):
    any_spec = pl.BlockSpec(memory_space=pl.ANY)
    return pl.pallas_call(
        join_low_body,
        name="join_cotangent",
        in_specs=[any_spec] * (len(blocks) + 1),
        out_specs=any_spec,
        out_shape=jax.ShapeDtypeStruct(shape, BF16),
        scratch_shapes=[pltpu.SemaphoreType.DMA((len(blocks), 2))],
        compiler_params=pltpu.CompilerParams(vmem_limit_bytes=1024 * 1024),
    )(*[hbm(block) for block in blocks], after)


def split_low_body(own_ref, other_ref, *out_refs):
    count = len(out_refs)
    low = lax.rem(lax.axis_index("mp"), count)
    high = lax.axis_index("mp") // count
    rows = out_refs[0].shape[1]
    for step in range(count):
        target = lax.rem(low + step, count)
        for side, place in ((0, high), (1, 1 - high)):
            start = pl.multiple_of((place * count + target) * rows, rows)
            total = own_ref[pl.ds(start, rows)].astype(F32) + other_ref[pl.ds(start, rows)].astype(F32)
            out_refs[step][side] = total.astype(BF16)


def sum_low_body(*refs):
    near_ref, far_ref = refs[-2:]
    for side, out_ref in enumerate((near_ref, far_ref)):
        total = refs[0][side].astype(F32)
        for ref in refs[1:-2]:
            total = total + ref[side].astype(F32)
        out_ref[...] = total.astype(BF16)


def grad_act_body(mine_ref, other_ref, w_ref, out_ref, rows_ref):
    @pl.when(pl.program_id(0) == 0)
    def _():
        join_halves(mine_ref, other_ref, rows_ref)

    out_ref[...] = dot(rows_ref[...], w_ref[...], NT)


def hidden_body(
    mine_ref, other_ref, w_ref, act_ref, hidden_ref, grad_ref, rows_ref
):
    join_halves(mine_ref, other_ref, rows_ref)

    for step in range(w_ref.shape[1] // 256):
        cols = slice(step * 256, (step + 1) * 256)
        pre = dot(rows_ref[...], w_ref[:, cols])
        cumul = 0.5 * (1.0 + lax.erf(pre * 0.7071067811865476))
        hidden_ref[:, cols] = (pre * cumul).astype(BF16)
        slope = cumul + pre * jnp.exp(-0.5 * pre * pre) * 0.3989422804014327
        grad_ref[:, cols] = (act_ref[:, cols] * slope).astype(BF16)


def grad_norm_body(start, rows_ref, w_ref, own_ref, other_ref):
    size = 512
    for step in range(own_ref.shape[1] // size):
        source = slice(start + step * size, start + (step + 1) * size)
        total = dot(rows_ref[...], w_ref[source, :], NT)
        put_halves(own_ref, other_ref, slice(step * size, (step + 1) * size), total)


def pair_body(*refs):
    *sides, out_ref, total_ref, sems = refs
    size = sides[0].shape[1]
    count = sems.shape[0]
    rows = out_ref.shape[0] // count
    moves = []
    for step in range(count):
        part = pl.ds(step * rows, rows)
        for index in range(len(sides) // 2):
            total = sides[2 * index][part].astype(F32) + sides[2 * index + 1][part].astype(F32)
            total_ref[part, index * size : (index + 1) * size] = total.astype(BF16)
        moves.append(
            pltpu.make_async_copy(total_ref.at[part], out_ref.at[part], sems.at[step])
        )
        moves[-1].start()
    for move in moves:
        move.wait()


def down_body(rows_ref, w_ref, own_ref, other_ref):
    put_halves(own_ref, other_ref, slice(None), dot(rows_ref[...], w_ref[...]))


def out_grad_body(mine_ref, other_ref, w_ref, pack_ref, rows_ref):
    join_halves(mine_ref, other_ref, rows_ref)
    half_rows = pack_ref.shape[1]
    grad = dot(rows_ref[...], w_ref[...], NT).astype(BF16)
    for slot in range(8):
        _, row, col = pack_place(slot, half_rows)
        pack_ref[slot] = grad[row : row + half_rows, col : col + HD]


def qkv_grad_body(base, pack_ref, w_ref, *refs):
    own_ref, other_ref, rows_ref, w_buf, sems = refs[-5:]
    half_rows = pack_ref.shape[1] // 5
    steps = sems.shape[0]
    size = w_buf.shape[1] // steps

    def move(step):
        source = pl.ds(base + step * size, size)
        cols = pl.ds(step * size, size)
        return pltpu.make_async_copy(w_ref.at[:, source, :], w_buf.at[:, cols, :], sems.at[step])

    for step in range(steps):
        move(step).start()
    for slot in range(8):
        _, row, col = pack_place(slot, half_rows)
        rows_ref[0, row : row + half_rows, col : col + HD] = pack_ref[slot, :half_rows]
    for slot in range(0, 8, 2):
        row, _, col = pack_place(slot, half_rows)
        for part in (1, 2):
            start = half_rows * (2 * part - 1)
            both = pack_ref[slot, start : start + 2 * half_rows].astype(F32) + pack_ref[
                slot + 1, start : start + 2 * half_rows
            ].astype(F32)
            rows_ref[part, row : row + 2 * half_rows, col : col + HD] = both.astype(BF16)

    for step in range(steps):
        move(step).wait()
        cols = slice(step * size, (step + 1) * size)
        total = dot(rows_ref[0], w_buf[0, cols, :], NT)
        for part in (1, 2):
            total = total + dot(rows_ref[part], w_buf[part, cols, :], NT)
        put_halves(own_ref, other_ref, cols, total)


def swap_section(data):
    return lax.ppermute(data, "section", [(0, 1), (1, 0)])


def exchange(data, axis):
    return lax.all_to_all(data, axis, 0, 0)


def by_columns(partial, half, width):
    sides = [partial(start) for start in (0, width // 2)]
    ins = []
    for own, other in sides:
        ins += [own, swap_section(other)]
    return pl.pallas_call(
        pair_body,
        name="pair",
        in_specs=[pl.BlockSpec(memory_space=pltpu.VMEM)] * len(ins),
        out_specs=pl.BlockSpec(memory_space=pl.ANY),
        out_shape=jax.ShapeDtypeStruct((half, width), BF16),
        scratch_shapes=[pltpu.VMEM((half, width), BF16), pltpu.SemaphoreType.DMA((4,))],
        compiler_params=pltpu.CompilerParams(vmem_limit_bytes=16 * 1024 * 1024),
    )(*ins)


def pair_sum(own, other):
    return (own.astype(F32) + swap_section(other).astype(F32)).astype(BF16)


def shift_high(data):
    size = lax.axis_size("mp")
    return lax.ppermute(data, "mp", [(i, (i + size // 2) % size) for i in range(size)])


def shift_low(data, step):
    size = lax.axis_size("mp") // 2
    pairs = [(h * size + i, h * size + (i + step) % size) for h in range(2) for i in range(size)]
    return lax.ppermute(data, "mp", pairs)


def per_device(bottleneck, qkv_weight, out_weight, up_weight, down_weight, cotangent):
    own_in = bottleneck[0]
    own_cot = cotangent[0]
    rows, width = own_in.shape
    group = lax.axis_size("mp")
    seq_size = lax.axis_size("seq")
    half = rows * group
    total_rows = 2 * half
    half_rows = half // 2
    head_cols = qkv_weight.shape[2]
    units = up_weight.shape[1]
    assert (total_rows // half) * (head_cols // HD) * 2 == seq_size == 8
    copies = ((group, rows, width), BF16)
    row_out = ((rows, width), BF16)
    halves = [((half, width), BF16)] * 2
    column_halves = [((half, width // 2), BF16)] * 2
    att_shape = ((seq_size, half_rows, HD), BF16)
    pack_shape = ((seq_size, 5 * half_rows, HD), BF16)
    big = 2 * total_rows * width * units
    joined = pltpu.VMEM((total_rows, width), BF16)

    (send,) = local_call(first_norm_body, "first_norm", [own_in], [copies])
    send, cot_near = lax.optimization_barrier((send, own_cot))
    cot_far = shift_high(cot_near)
    weight = fetch(qkv_weight, send, "fetch_qkv")
    mine, cot_far = lax.optimization_barrier((exchange(send, "mp"), cot_far))
    mine = mine.reshape(half, width)
    (send,) = local_call(
        qkv_body,
        "qkv",
        [mine, swap_section(mine), weight],
        [pack_shape],
        [joined],
        flops=2 * total_rows * width * 3 * head_cols,
    )
    send, cot_near, cot_far = lax.optimization_barrier((send, cot_near, cot_far))
    cot_two = jnp.stack([cot_near, cot_far])
    pack = exchange(send, "seq")
    cot_shifted = [shift_low(cot_two, step) for step in range(1, group // 2)]
    att, lse = local_call(
        attention_body,
        "attention",
        [pack],
        [att_shape, ((4, 1, 2 * half_rows), F32)],
        flops=4 * half * half * 8 * HD,
    )
    weight = fetch(out_weight, att, "fetch_out")
    got = exchange(att, "seq")
    cot_mine = join_low([cot_two, *cot_shifted], att, (half, width))
    cots = [cot_mine, swap_section(cot_mine)]

    def attn_out(start):
        return local_call(
            functools.partial(out_body, start),
            "attn_out",
            [got, weight],
            column_halves,
            [pltpu.VMEM((total_rows, head_cols), BF16)],
            after=[cot_mine],
        )

    send = by_columns(attn_out, half, width).reshape(group, rows, width)
    unit_block = units // 4
    unit_spec = pl.BlockSpec((total_rows, unit_block), lambda j: (0, j))
    (grad_act,) = kernel_call(
        grad_act_body,
        "grad_act",
        (4,),
        [
            *[(cot, None) for cot in cots],
            (hbm(down_weight), pl.BlockSpec((unit_block, width), lambda j: (j, 0))),
        ],
        [((total_rows, units), F32, unit_spec)],
        [joined],
        after=[send],
        flops=big,
        nbytes=2 * width * units,
    )
    parts = exchange(send, "mp")
    resid, send = local_call(
        second_norm_body, "second_norm", [parts, own_in], [row_out, copies], after=[grad_act]
    )
    mine = exchange(send, "mp").reshape(half, width)
    weight = fetch(up_weight, send, "fetch_up")
    hidden, grad_hidden = local_call(
        hidden_body,
        "hidden",
        [mine, swap_section(mine), weight, grad_act],
        [((total_rows, units), BF16)] * 2,
        [joined],
        flops=big,
    )

    def grad_norm_two(start):
        return local_call(
            functools.partial(grad_norm_body, start),
            "grad_norm_two",
            [grad_hidden, weight],
            column_halves,
        )

    send = by_columns(grad_norm_two, half, width).reshape(group, rows, width)
    block = width // 8
    block_spec = pl.BlockSpec((half, block), lambda j: (0, j))
    own, other = kernel_call(
        down_body,
        "down",
        (8,),
        [(hidden, None), (hbm(down_weight), pl.BlockSpec((units, block), lambda j: (0, j)))],
        [(shape, dtype, block_spec) for shape, dtype in halves],
        after=[send],
        flops=big,
        nbytes=2 * width * units,
    )
    parts = exchange(send, "mp")
    grad_resid, send, mark = local_call(
        resid_grad_body,
        "resid_grad",
        [parts, resid, own_cot],
        [row_out, copies, ((8, 128), F32)],
        after=[own],
    )
    weight = fetch(out_weight, send, "fetch_out_again")
    other, mark = lax.optimization_barrier((other, mark))
    sums_low = local_call(
        split_low_body,
        "split_sums",
        [own, swap_section(other)],
        [((2, rows, width), BF16)] * (group // 2),
    )
    mine, *sums_low = lax.optimization_barrier((exchange(send, "mp"), *sums_low))
    mine = mine.reshape(half, width)
    (send,) = local_call(
        out_grad_body,
        "attn_out_grad",
        [mine, swap_section(mine), weight],
        [att_shape],
        [joined],
        after=[mark],
        flops=2 * total_rows * width * head_cols,
    )
    grad_att = exchange(send, "seq")
    (send,) = local_call(
        attention_grad_body,
        "attention_grad",
        [pack, att, lse, grad_att],
        [pack_shape],
        flops=10 * half * half * 8 * HD,
    )
    send, *sums_low = lax.optimization_barrier((send, *sums_low))
    shifted = [shift_low(sums_low[step], step) for step in range(1, group // 2)]
    sum_near, sum_far = local_call(
        sum_low_body, "join_sums", [sums_low[0], *shifted], [row_out] * 2
    )
    sum_far = shift_high(sum_far)
    got = exchange(send, "seq")
    vmem = pl.BlockSpec(memory_space=pltpu.VMEM)

    def qkv_grad(start):
        after = shifted if start == 0 else [sum_near]
        return pl.pallas_call(
            functools.partial(qkv_grad_body, start),
            name="qkv_grad",
            in_specs=[vmem, pl.BlockSpec(memory_space=pltpu.HBM)]
            + [pl.BlockSpec(memory_space=pl.ANY)] * len(after),
            out_specs=[vmem] * 2,
            out_shape=[jax.ShapeDtypeStruct(shape, dtype) for shape, dtype in column_halves],
            scratch_shapes=[
                pltpu.VMEM((3, total_rows, head_cols), BF16),
                pltpu.VMEM((3, width // 2, head_cols), BF16),
                pltpu.SemaphoreType.DMA((4,)),
            ],
            compiler_params=pltpu.CompilerParams(vmem_limit_bytes=16 * 1024 * 1024),
            cost_estimate=pl.CostEstimate(flops=0, bytes_accessed=0, transcendentals=0),
        )(got, hbm(qkv_weight), *after)

    parts = exchange(by_columns(qkv_grad, half, width).reshape(group, rows, width), "mp")
    grad_input, block_out = local_call(
        input_grad_body,
        "input_grad",
        [parts],
        [row_out, row_out],
        late=[hbm(own_in), grad_resid, resid, sum_near, sum_far],
    )
    return (block_out[None], grad_input[None])


def solution(mesh):
    in_specs = (
        P("section", ("seq", "mp"), None),
        P(None, None, ("section", "mp")),
        P(("section", "mp"), None),
        P(None, ("section", "mp")),
        P(("section", "mp"), None),
        P("section", ("seq", "mp"), None),
    )
    out_specs = (P("section", ("seq", "mp"), None), P("section", ("seq", "mp"), None))
    return jax.shard_map(
        per_device, mesh=mesh, in_specs=in_specs, out_specs=out_specs, check_vma=False
    )
```

```python
import functools
import math

import jax
import jax.numpy as jnp
from jax import lax
from jax.experimental import pallas as pl
from jax.experimental.pallas import tpu as pltpu
from jax.sharding import PartitionSpec as P

HD = 128
norm_eps = 1e-06
F32 = jnp.float32
BF16 = jnp.bfloat16
NT = (((1,), (1,)), ((), ()))
NN = (((1,), (0,)), ((), ()))
TN = (((0,), (0,)), ((), ()))


def dot(lhs, rhs, dims=NN):
    return lax.dot_general(lhs, rhs, dims, preferred_element_type=F32)


def whole(shape):
    rank = len(shape)
    return pl.BlockSpec(shape, lambda *ids: (0,) * rank)


def kernel_call(body, name, grid, ins, outs, scratch=(), after=(), flops=0, nbytes=0):
    count = len(ins)

    def run(*refs):
        body(*refs[:count], *refs[count + len(after) :])

    in_specs = [whole(arr.shape) if spec is None else spec for arr, spec in ins]
    in_specs += [pl.BlockSpec(memory_space=pl.ANY)] * len(after)
    out_specs = [whole(shape) if spec is None else spec for shape, _, spec in outs]
    return pl.pallas_call(
        run,
        name=name,
        grid=grid,
        in_specs=in_specs,
        out_specs=out_specs,
        out_shape=[jax.ShapeDtypeStruct(shape, dtype) for shape, dtype, _ in outs],
        scratch_shapes=list(scratch),
        compiler_params=pltpu.CompilerParams(vmem_limit_bytes=16 * 1024 * 1024),
        cost_estimate=pl.CostEstimate(flops=flops, bytes_accessed=nbytes, transcendentals=0),
    )(*[arr for arr, _ in ins], *after)


def hbm(array):
    return pltpu.with_memory_space_constraint(array, pltpu.HBM)


def fetch(weight, after, name, part=0, parts=1):
    rows = weight.shape[0] // parts

    def fetch_body(src_ref, after_ref, dst_ref):
        pltpu.sync_copy(src_ref.at[pl.ds(part * rows, rows)], dst_ref)

    return pl.pallas_call(
        fetch_body,
        name=name,
        in_specs=[pl.BlockSpec(memory_space=pltpu.HBM), pl.BlockSpec(memory_space=pl.ANY)],
        out_specs=pl.BlockSpec(memory_space=pltpu.VMEM),
        out_shape=pltpu.VMEM((rows,) + weight.shape[1:], weight.dtype),
        compiler_params=pltpu.CompilerParams(vmem_limit_bytes=1024 * 1024),
        cost_estimate=pl.CostEstimate(
            flops=0, bytes_accessed=2 * weight.size // parts, transcendentals=0
        ),
    )(hbm(weight), after)


def local_call(
    body, name, ins, outs, scratch=(), after=(), late=(), aliases=None, flops=0, nbytes=0
):
    vmem = pl.BlockSpec(memory_space=pltpu.VMEM)
    count, extra = len(ins), len(late)

    def run(*refs):
        sources = refs[count : count + extra]
        rest = refs[count + extra + len(after) :]
        if not extra:
            body(*refs[:count], *rest)
            return
        buffers, sems = rest[-1 - extra : -1], rest[-1]
        moves = [
            pltpu.make_async_copy(source, buffer, sems.at[index])
            for index, (source, buffer) in enumerate(zip(sources, buffers))
        ]
        for move in moves:
            move.start()

        def wait():
            for move in moves:
                move.wait()

        body(*refs[:count], *buffers, *rest[: -1 - extra], wait)

    scratch = list(scratch)
    if extra:
        scratch += [pltpu.VMEM(arr.shape, arr.dtype) for arr in late]
        scratch.append(pltpu.SemaphoreType.DMA((extra,)))
    return pl.pallas_call(
        run,
        name=name,
        in_specs=[vmem] * count + [pl.BlockSpec(memory_space=pl.ANY)] * (extra + len(after)),
        out_specs=[
            vmem if len(out) == 2 else pl.BlockSpec(memory_space=pl.ANY) for out in outs
        ],
        out_shape=[jax.ShapeDtypeStruct(*out[:2]) for out in outs],
        scratch_shapes=scratch,
        input_output_aliases=aliases or {},
        compiler_params=pltpu.CompilerParams(vmem_limit_bytes=16 * 1024 * 1024),
        cost_estimate=pl.CostEstimate(flops=flops, bytes_accessed=nbytes, transcendentals=0),
    )(*ins, *late, *after)


def row_norm(rows):
    mean = jnp.mean(rows, axis=-1, keepdims=True)
    centered = rows - mean
    inv_std = lax.rsqrt(jnp.mean(centered * centered, axis=-1, keepdims=True) + norm_eps)
    return centered * inv_std, inv_std


def row_norm_backward(normed, inv_std, grad):
    mean_grad = jnp.mean(grad, axis=-1, keepdims=True)
    mean_mix = jnp.mean(grad * normed, axis=-1, keepdims=True)
    return inv_std * (grad - mean_grad - normed * mean_mix)


def add_parts(parts_ref):
    total = parts_ref[0].astype(F32)
    for index in range(1, parts_ref.shape[0]):
        total = total + parts_ref[index].astype(F32)
    return total


def fill_copies(copies_ref, rows):
    for index in range(copies_ref.shape[0]):
        copies_ref[index] = rows


def first_norm_body(in_ref, copies_ref):
    normed, _ = row_norm(in_ref[...].astype(F32))
    fill_copies(copies_ref, normed.astype(BF16))


def second_norm_body(parts_ref, in_ref, resid_ref, copies_ref):
    total = add_parts(parts_ref)
    resid = (in_ref[...].astype(F32) + total).astype(BF16)
    resid_ref[...] = resid
    normed, _ = row_norm(resid.astype(F32))
    fill_copies(copies_ref, normed.astype(BF16))


def resid_grad_body(parts_ref, resid_ref, cot_ref, grad_ref, copies_ref, mark_ref):
    mark_ref[...] = jnp.zeros_like(mark_ref)
    total = add_parts(parts_ref)
    normed, inv_std = row_norm(resid_ref[...].astype(F32))
    grad = row_norm_backward(normed, inv_std, total)
    grad = (cot_ref[...].astype(F32) + grad).astype(BF16)
    grad_ref[...] = grad
    fill_copies(copies_ref, grad)


def input_grad_body(
    parts_ref, in_ref, grad_ref, resid_ref, near_ref, far_ref, out_ref, block_ref, wait
):
    total = add_parts(parts_ref)
    wait()
    ffn = near_ref[...].astype(F32) + far_ref[...].astype(F32)
    block_ref[...] = (resid_ref[...].astype(F32) + ffn).astype(BF16)
    normed, inv_std = row_norm(in_ref[...].astype(F32))
    grad = row_norm_backward(normed, inv_std, total)
    out_ref[...] = (grad_ref[...].astype(F32) + grad).astype(BF16)


def pack_place(slot, half_rows):
    image, head, half = slot // 4, (slot // 2) % 2, slot % 2
    row = image * 2 * half_rows
    return row, row + half * half_rows, head * HD


def join_halves(mine_ref, other_ref, rows_ref):
    half = mine_ref.shape[0]
    rows_ref[:half] = mine_ref[...]
    rows_ref[half:] = other_ref[...]


def qkv_body(mine_ref, other_ref, w_ref, send_ref, rows_ref, pack_ref, sems):
    join_halves(mine_ref, other_ref, rows_ref)
    half_rows = pack_ref.shape[1] // 5
    moves = []
    for part in range(3):
        acc = dot(rows_ref[...], w_ref[part]).astype(BF16)
        start = half_rows * max(2 * part - 1, 0)
        size = half_rows * min(part + 1, 2)
        for slot in range(8):
            image_row, row, col = pack_place(slot, half_rows)
            first = row if part == 0 else image_row
            pack_ref[slot, start : start + size] = acc[first : first + size, col : col + HD]
        place = pl.ds(start, size)
        moves.append(
            pltpu.make_async_copy(pack_ref.at[:, place], send_ref.at[:, place], sems.at[part])
        )
        moves[-1].start()
    for move in moves:
        move.wait()


def attention_body(pack_ref, att_ref, lse_ref):
    half_rows = att_ref.shape[1]
    keys = pack_ref[:, half_rows : 3 * half_rows, :].reshape(-1, HD)
    values = pack_ref[:, 3 * half_rows :, :].reshape(-1, HD)
    scale = 1.0 / math.sqrt(HD)
    for chunk in range(4):
        queries = pack_ref[2 * chunk : 2 * chunk + 2, :half_rows, :].reshape(-1, HD)
        scores = dot(keys, queries, NT) * scale
        row_max = jnp.max(scores, axis=0, keepdims=True)
        weights = jnp.exp(scores - row_max)
        total = jnp.sum(weights, axis=0, keepdims=True)
        lse_ref[chunk] = row_max + jnp.log(total)
        mixed = dot(values, weights.astype(BF16), TN) / total
        att_ref[2 * chunk : 2 * chunk + 2] = mixed.T.astype(BF16).reshape(2, half_rows, HD)


def attention_grad_body(pack_ref, att_ref, lse_ref, grad_ref, send_ref, out_ref, sems):
    half_rows = att_ref.shape[1]
    scale = 1.0 / math.sqrt(HD)
    queries = pack_ref[:, :half_rows, :].reshape(-1, HD)
    grads = grad_ref[...].reshape(-1, HD)
    mix = grads.astype(F32) * att_ref[...].reshape(-1, HD).astype(F32)
    delta = jnp.sum(mix.T, axis=0, keepdims=True)
    lse = jnp.concatenate([lse_ref[chunk] for chunk in range(4)], axis=1)
    query_total = None
    moves = []
    for slot in range(8):
        keys = pack_ref[slot, half_rows : 3 * half_rows, :]
        values = pack_ref[slot, 3 * half_rows :, :]
        probs = jnp.exp(dot(keys, queries, NT) * scale - lse)
        grad_probs = dot(values, grads, NT)
        grad_scores = (probs * (grad_probs - delta) * scale).astype(BF16)
        out_ref[slot, half_rows : 3 * half_rows] = dot(grad_scores, queries).astype(BF16)
        out_ref[slot, 3 * half_rows :] = dot(probs.astype(BF16), grads).astype(BF16)
        term = dot(keys, grad_scores, TN)
        query_total = term if query_total is None else query_total + term
        part = pl.ds(half_rows, 4 * half_rows)
        moves.append(
            pltpu.make_async_copy(
                out_ref.at[slot, part], send_ref.at[slot, part], sems.at[slot]
            )
        )
        moves[-1].start()
    out_ref[:, :half_rows] = query_total.T.astype(BF16).reshape(8, half_rows, HD)
    part = pl.ds(0, half_rows)
    moves.append(pltpu.make_async_copy(out_ref.at[:, part], send_ref.at[:, part], sems.at[8]))
    moves[-1].start()
    for move in moves:
        move.wait()


def put_halves(own_ref, other_ref, cols, total):
    half = own_ref.shape[0]
    own_ref[:, cols] = total[:half].astype(BF16)
    other_ref[:, cols] = total[half:].astype(BF16)


def out_body(start, att_ref, w_ref, own_ref, other_ref, rows_ref):
    half_rows = att_ref.shape[1]
    for slot in range(8):
        _, row, col = pack_place(slot, half_rows)
        rows_ref[row : row + half_rows, col : col + HD] = att_ref[slot]
    size = 512
    for step in range(own_ref.shape[1] // size):
        cols = slice(start + step * size, start + (step + 1) * size)
        total = dot(rows_ref[...], w_ref[:, cols])
        put_halves(own_ref, other_ref, slice(step * size, (step + 1) * size), total)


def join_low_body(*refs):
    *block_refs, _, out_ref, sems = refs
    count = len(block_refs)
    low = lax.rem(lax.axis_index("mp"), count)
    high = lax.axis_index("mp") // count
    rows = block_refs[0].shape[1]
    moves = []
    for step in range(count):
        source = lax.rem(low + count - step, count)
        for side, place in ((0, high), (1, 1 - high)):
            start = pl.multiple_of((place * count + source) * rows, rows)
            moves.append(
                pltpu.make_async_copy(
                    block_refs[step].at[side], out_ref.at[pl.ds(start, rows)], sems.at[step, side]
                )
            )
    for move in moves:
        move.start()
    for move in moves:
        move.wait()


def join_low(blocks, after, shape):
    any_spec = pl.BlockSpec(memory_space=pl.ANY)
    return pl.pallas_call(
        join_low_body,
        name="join_cotangent",
        in_specs=[any_spec] * (len(blocks) + 1),
        out_specs=any_spec,
        out_shape=jax.ShapeDtypeStruct(shape, BF16),
        scratch_shapes=[pltpu.SemaphoreType.DMA((len(blocks), 2))],
        compiler_params=pltpu.CompilerParams(vmem_limit_bytes=1024 * 1024),
    )(*[hbm(block) for block in blocks], after)


def split_low_body(own_ref, other_ref, *out_refs):
    count = len(out_refs)
    low = lax.rem(lax.axis_index("mp"), count)
    high = lax.axis_index("mp") // count
    rows = out_refs[0].shape[1]
    for step in range(count):
        target = lax.rem(low + step, count)
        for side, place in ((0, high), (1, 1 - high)):
            start = pl.multiple_of((place * count + target) * rows, rows)
            total = own_ref[pl.ds(start, rows)].astype(F32) + other_ref[pl.ds(start, rows)].astype(F32)
            out_refs[step][side] = total.astype(BF16)


def sum_low_body(*refs):
    near_ref, far_ref = refs[-2:]
    for side, out_ref in enumerate((near_ref, far_ref)):
        total = refs[0][side].astype(F32)
        for ref in refs[1:-2]:
            total = total + ref[side].astype(F32)
        out_ref[...] = total.astype(BF16)


def grad_act_body(mine_ref, other_ref, w_ref, out_ref, rows_ref):
    @pl.when(pl.program_id(0) == 0)
    def _():
        join_halves(mine_ref, other_ref, rows_ref)

    out_ref[...] = dot(rows_ref[...], w_ref[...], NT)


def hidden_body(
    mine_ref, other_ref, w_ref, act_ref, hidden_ref, grad_ref, rows_ref
):
    join_halves(mine_ref, other_ref, rows_ref)

    for step in range(w_ref.shape[1] // 256):
        cols = slice(step * 256, (step + 1) * 256)
        pre = dot(rows_ref[...], w_ref[:, cols])
        cumul = 0.5 * (1.0 + lax.erf(pre * 0.7071067811865476))
        hidden_ref[:, cols] = (pre * cumul).astype(BF16)
        slope = cumul + pre * jnp.exp(-0.5 * pre * pre) * 0.3989422804014327
        grad_ref[:, cols] = (act_ref[:, cols] * slope).astype(BF16)


def grad_norm_body(start, rows_ref, w_ref, own_ref, other_ref):
    size = 512
    for step in range(own_ref.shape[1] // size):
        source = slice(start + step * size, start + (step + 1) * size)
        total = dot(rows_ref[...], w_ref[source, :], NT)
        put_halves(own_ref, other_ref, slice(step * size, (step + 1) * size), total)


def pair_body(*refs):
    *sides, out_ref, total_ref, sems = refs
    size = sides[0].shape[1]
    count = sems.shape[0]
    rows = out_ref.shape[0] // count
    moves = []
    for step in range(count):
        part = pl.ds(step * rows, rows)
        for index in range(len(sides) // 2):
            total = sides[2 * index][part].astype(F32) + sides[2 * index + 1][part].astype(F32)
            total_ref[part, index * size : (index + 1) * size] = total.astype(BF16)
        moves.append(
            pltpu.make_async_copy(total_ref.at[part], out_ref.at[part], sems.at[step])
        )
        moves[-1].start()
    for move in moves:
        move.wait()


def down_body(rows_ref, w_ref, own_ref, other_ref):
    put_halves(own_ref, other_ref, slice(None), dot(rows_ref[...], w_ref[...]))


def out_grad_body(mine_ref, other_ref, w_ref, pack_ref, rows_ref):
    join_halves(mine_ref, other_ref, rows_ref)
    half_rows = pack_ref.shape[1]
    grad = dot(rows_ref[...], w_ref[...], NT).astype(BF16)
    for slot in range(8):
        _, row, col = pack_place(slot, half_rows)
        pack_ref[slot] = grad[row : row + half_rows, col : col + HD]


def qkv_grad_body(base, pack_ref, w_ref, *refs):
    own_ref, other_ref, rows_ref, w_buf, sems = refs[-5:]
    half_rows = pack_ref.shape[1] // 5
    steps = sems.shape[0]
    size = w_buf.shape[1] // steps

    def move(step):
        source = pl.ds(base + step * size, size)
        cols = pl.ds(step * size, size)
        return pltpu.make_async_copy(w_ref.at[:, source, :], w_buf.at[:, cols, :], sems.at[step])

    for step in range(steps):
        move(step).start()
    for slot in range(8):
        _, row, col = pack_place(slot, half_rows)
        rows_ref[0, row : row + half_rows, col : col + HD] = pack_ref[slot, :half_rows]
    for slot in range(0, 8, 2):
        row, _, col = pack_place(slot, half_rows)
        for part in (1, 2):
            start = half_rows * (2 * part - 1)
            both = pack_ref[slot, start : start + 2 * half_rows].astype(F32) + pack_ref[
                slot + 1, start : start + 2 * half_rows
            ].astype(F32)
            rows_ref[part, row : row + 2 * half_rows, col : col + HD] = both.astype(BF16)

    for step in range(steps):
        move(step).wait()
        cols = slice(step * size, (step + 1) * size)
        total = dot(rows_ref[0], w_buf[0, cols, :], NT)
        for part in (1, 2):
            total = total + dot(rows_ref[part], w_buf[part, cols, :], NT)
        put_halves(own_ref, other_ref, cols, total)


def swap_section(data):
    return lax.ppermute(data, "section", [(0, 1), (1, 0)])


def exchange(data, axis):
    return lax.all_to_all(data, axis, 0, 0)


def by_columns(partial, half, width):
    sides = [partial(start) for start in (0, width // 2)]
    ins = []
    for own, other in sides:
        ins += [own, swap_section(other)]
    return pl.pallas_call(
        pair_body,
        name="pair",
        in_specs=[pl.BlockSpec(memory_space=pltpu.VMEM)] * len(ins),
        out_specs=pl.BlockSpec(memory_space=pl.ANY),
        out_shape=jax.ShapeDtypeStruct((half, width), BF16),
        scratch_shapes=[pltpu.VMEM((half, width), BF16), pltpu.SemaphoreType.DMA((4,))],
        compiler_params=pltpu.CompilerParams(vmem_limit_bytes=16 * 1024 * 1024),
    )(*ins)


def pair_sum(own, other):
    return (own.astype(F32) + swap_section(other).astype(F32)).astype(BF16)


def shift_high(data):
    size = lax.axis_size("mp")
    return lax.ppermute(data, "mp", [(i, (i + size // 2) % size) for i in range(size)])


def shift_low(data, step):
    size = lax.axis_size("mp") // 2
    pairs = [(h * size + i, h * size + (i + step) % size) for h in range(2) for i in range(size)]
    return lax.ppermute(data, "mp", pairs)


def per_device(bottleneck, qkv_weight, out_weight, up_weight, down_weight, cotangent):
    own_in = bottleneck[0]
    own_cot = cotangent[0]
    rows, width = own_in.shape
    group = lax.axis_size("mp")
    seq_size = lax.axis_size("seq")
    half = rows * group
    total_rows = 2 * half
    half_rows = half // 2
    head_cols = qkv_weight.shape[2]
    units = up_weight.shape[1]
    assert (total_rows // half) * (head_cols // HD) * 2 == seq_size == 8
    copies = ((group, rows, width), BF16)
    row_out = ((rows, width), BF16)
    halves = [((half, width), BF16)] * 2
    column_halves = [((half, width // 2), BF16)] * 2
    att_shape = ((seq_size, half_rows, HD), BF16)
    pack_shape = ((seq_size, 5 * half_rows, HD), BF16)
    big = 2 * total_rows * width * units
    joined = pltpu.VMEM((total_rows, width), BF16)

    (send,) = local_call(first_norm_body, "first_norm", [own_in], [copies])
    send, cot_near = lax.optimization_barrier((send, own_cot))
    cot_far = shift_high(cot_near)
    weight = fetch(qkv_weight, send, "fetch_qkv")
    mine, cot_far = lax.optimization_barrier((exchange(send, "mp"), cot_far))
    mine = mine.reshape(half, width)
    (send,) = local_call(
        qkv_body,
        "qkv",
        [mine, swap_section(mine), weight],
        [pack_shape + ("hbm",)],
        [joined, pltpu.VMEM(*pack_shape), pltpu.SemaphoreType.DMA((3,))],
        flops=2 * total_rows * width * 3 * head_cols,
    )
    send, cot_near, cot_far = lax.optimization_barrier((send, cot_near, cot_far))
    cot_two = jnp.stack([cot_near, cot_far])
    pack = exchange(send, "seq")
    cot_shifted = [shift_low(cot_two, step) for step in range(1, group // 2)]
    att, lse = local_call(
        attention_body,
        "attention",
        [pack],
        [att_shape, ((4, 1, 2 * half_rows), F32)],
        flops=4 * half * half * 8 * HD,
    )
    weight = fetch(out_weight, att, "fetch_out")
    got = exchange(att, "seq")
    cot_mine = join_low([cot_two, *cot_shifted], att, (half, width))
    cots = [cot_mine, swap_section(cot_mine)]

    def attn_out(start):
        return local_call(
            functools.partial(out_body, start),
            "attn_out",
            [got, weight],
            column_halves,
            [pltpu.VMEM((total_rows, head_cols), BF16)],
            after=[cot_mine],
        )

    send = by_columns(attn_out, half, width).reshape(group, rows, width)
    unit_block = units // 4
    unit_spec = pl.BlockSpec((total_rows, unit_block), lambda j: (0, j))
    (grad_act,) = kernel_call(
        grad_act_body,
        "grad_act",
        (4,),
        [
            *[(cot, None) for cot in cots],
            (hbm(down_weight), pl.BlockSpec((unit_block, width), lambda j: (j, 0))),
        ],
        [((total_rows, units), F32, unit_spec)],
        [joined],
        after=[send],
        flops=big,
        nbytes=2 * width * units,
    )
    parts = exchange(send, "mp")
    resid, send = local_call(
        second_norm_body, "second_norm", [parts, own_in], [row_out, copies], after=[grad_act]
    )
    mine = exchange(send, "mp").reshape(half, width)
    weight = fetch(up_weight, send, "fetch_up")
    hidden, grad_hidden = local_call(
        hidden_body,
        "hidden",
        [mine, swap_section(mine), weight, grad_act],
        [((total_rows, units), BF16)] * 2,
        [joined],
        flops=big,
    )

    def grad_norm_two(start):
        return local_call(
            functools.partial(grad_norm_body, start),
            "grad_norm_two",
            [grad_hidden, weight],
            column_halves,
        )

    send = by_columns(grad_norm_two, half, width).reshape(group, rows, width)
    block = width // 8
    block_spec = pl.BlockSpec((half, block), lambda j: (0, j))
    own, other = kernel_call(
        down_body,
        "down",
        (8,),
        [(hidden, None), (hbm(down_weight), pl.BlockSpec((units, block), lambda j: (0, j)))],
        [(shape, dtype, block_spec) for shape, dtype in halves],
        after=[send],
        flops=big,
        nbytes=2 * width * units,
    )
    parts = exchange(send, "mp")
    grad_resid, send, mark = local_call(
        resid_grad_body,
        "resid_grad",
        [parts, resid, own_cot],
        [row_out, copies, ((8, 128), F32)],
        after=[own],
    )
    weight = fetch(out_weight, send, "fetch_out_again")
    other, mark = lax.optimization_barrier((other, mark))
    sums_low = local_call(
        split_low_body,
        "split_sums",
        [own, swap_section(other)],
        [((2, rows, width), BF16)] * (group // 2),
    )
    mine, *sums_low = lax.optimization_barrier((exchange(send, "mp"), *sums_low))
    mine = mine.reshape(half, width)
    (send,) = local_call(
        out_grad_body,
        "attn_out_grad",
        [mine, swap_section(mine), weight],
        [att_shape],
        [joined],
        after=[mark],
        flops=2 * total_rows * width * head_cols,
    )
    grad_att = exchange(send, "seq")
    (send,) = local_call(
        attention_grad_body,
        "attention_grad",
        [pack, att, lse, grad_att],
        [pack_shape + ("hbm",)],
        [pltpu.VMEM(*pack_shape), pltpu.SemaphoreType.DMA((9,))],
        flops=10 * half * half * 8 * HD,
    )
    send, *sums_low = lax.optimization_barrier((send, *sums_low))
    shifted = [shift_low(sums_low[step], step) for step in range(1, group // 2)]
    sum_near, sum_far = local_call(
        sum_low_body, "join_sums", [sums_low[0], *shifted], [row_out] * 2
    )
    sum_far = shift_high(sum_far)
    got = exchange(send, "seq")
    vmem = pl.BlockSpec(memory_space=pltpu.VMEM)

    def qkv_grad(start):
        after = shifted if start == 0 else [sum_near]
        return pl.pallas_call(
            functools.partial(qkv_grad_body, start),
            name="qkv_grad",
            in_specs=[vmem, pl.BlockSpec(memory_space=pltpu.HBM)]
            + [pl.BlockSpec(memory_space=pl.ANY)] * len(after),
            out_specs=[vmem] * 2,
            out_shape=[jax.ShapeDtypeStruct(shape, dtype) for shape, dtype in column_halves],
            scratch_shapes=[
                pltpu.VMEM((3, total_rows, head_cols), BF16),
                pltpu.VMEM((3, width // 2, head_cols), BF16),
                pltpu.SemaphoreType.DMA((4,)),
            ],
            compiler_params=pltpu.CompilerParams(vmem_limit_bytes=16 * 1024 * 1024),
            cost_estimate=pl.CostEstimate(flops=0, bytes_accessed=0, transcendentals=0),
        )(got, hbm(qkv_weight), *after)

    parts = exchange(by_columns(qkv_grad, half, width).reshape(group, rows, width), "mp")
    grad_input, block_out = local_call(
        input_grad_body,
        "input_grad",
        [parts],
        [row_out, row_out],
        late=[hbm(own_in), grad_resid, resid, sum_near, sum_far],
    )
    return (block_out[None], grad_input[None])


def solution(mesh):
    in_specs = (
        P("section", ("seq", "mp"), None),
        P(None, None, ("section", "mp")),
        P(("section", "mp"), None),
        P(None, ("section", "mp")),
        P(("section", "mp"), None),
        P("section", ("seq", "mp"), None),
    )
    out_specs = (P("section", ("seq", "mp"), None), P("section", ("seq", "mp"), None))
    return jax.shard_map(
        per_device, mesh=mesh, in_specs=in_specs, out_specs=out_specs, check_vma=False
    )
```

```python
import functools
import math

import jax
import jax.numpy as jnp
from jax import lax
from jax.experimental import pallas as pl
from jax.experimental.pallas import tpu as pltpu
from jax.sharding import PartitionSpec as P

HD = 128
norm_eps = 1e-06
F32 = jnp.float32
BF16 = jnp.bfloat16
NT = (((1,), (1,)), ((), ()))
NN = (((1,), (0,)), ((), ()))
TN = (((0,), (0,)), ((), ()))


def dot(lhs, rhs, dims=NN):
    return lax.dot_general(lhs, rhs, dims, preferred_element_type=F32)


def whole(shape):
    rank = len(shape)
    return pl.BlockSpec(shape, lambda *ids: (0,) * rank)


def kernel_call(body, name, grid, ins, outs, scratch=(), after=(), flops=0, nbytes=0):
    count = len(ins)

    def run(*refs):
        body(*refs[:count], *refs[count + len(after) :])

    in_specs = [whole(arr.shape) if spec is None else spec for arr, spec in ins]
    in_specs += [pl.BlockSpec(memory_space=pl.ANY)] * len(after)
    out_specs = [whole(shape) if spec is None else spec for shape, _, spec in outs]
    return pl.pallas_call(
        run,
        name=name,
        grid=grid,
        in_specs=in_specs,
        out_specs=out_specs,
        out_shape=[jax.ShapeDtypeStruct(shape, dtype) for shape, dtype, _ in outs],
        scratch_shapes=list(scratch),
        compiler_params=pltpu.CompilerParams(vmem_limit_bytes=16 * 1024 * 1024),
        cost_estimate=pl.CostEstimate(flops=flops, bytes_accessed=nbytes, transcendentals=0),
    )(*[arr for arr, _ in ins], *after)


def hbm(array):
    return pltpu.with_memory_space_constraint(array, pltpu.HBM)


def fetch(weight, after, name, part=0, parts=1):
    rows = weight.shape[0] // parts

    def fetch_body(src_ref, after_ref, dst_ref):
        pltpu.sync_copy(src_ref.at[pl.ds(part * rows, rows)], dst_ref)

    return pl.pallas_call(
        fetch_body,
        name=name,
        in_specs=[pl.BlockSpec(memory_space=pltpu.HBM), pl.BlockSpec(memory_space=pl.ANY)],
        out_specs=pl.BlockSpec(memory_space=pltpu.VMEM),
        out_shape=pltpu.VMEM((rows,) + weight.shape[1:], weight.dtype),
        compiler_params=pltpu.CompilerParams(vmem_limit_bytes=1024 * 1024),
        cost_estimate=pl.CostEstimate(
            flops=0, bytes_accessed=2 * weight.size // parts, transcendentals=0
        ),
    )(hbm(weight), after)


def local_call(
    body, name, ins, outs, scratch=(), after=(), late=(), aliases=None, flops=0, nbytes=0
):
    vmem = pl.BlockSpec(memory_space=pltpu.VMEM)
    count, extra = len(ins), len(late)

    def run(*refs):
        sources = refs[count : count + extra]
        rest = refs[count + extra + len(after) :]
        if not extra:
            body(*refs[:count], *rest)
            return
        buffers, sems = rest[-1 - extra : -1], rest[-1]
        moves = [
            pltpu.make_async_copy(source, buffer, sems.at[index])
            for index, (source, buffer) in enumerate(zip(sources, buffers))
        ]
        for move in moves:
            move.start()

        def wait():
            for move in moves:
                move.wait()

        body(*refs[:count], *buffers, *rest[: -1 - extra], wait)

    scratch = list(scratch)
    if extra:
        scratch += [pltpu.VMEM(arr.shape, arr.dtype) for arr in late]
        scratch.append(pltpu.SemaphoreType.DMA((extra,)))
    return pl.pallas_call(
        run,
        name=name,
        in_specs=[vmem] * count + [pl.BlockSpec(memory_space=pl.ANY)] * (extra + len(after)),
        out_specs=[
            vmem if len(out) == 2 else pl.BlockSpec(memory_space=pl.ANY) for out in outs
        ],
        out_shape=[jax.ShapeDtypeStruct(*out[:2]) for out in outs],
        scratch_shapes=scratch,
        input_output_aliases=aliases or {},
        compiler_params=pltpu.CompilerParams(vmem_limit_bytes=16 * 1024 * 1024),
        cost_estimate=pl.CostEstimate(flops=flops, bytes_accessed=nbytes, transcendentals=0),
    )(*ins, *late, *after)


def row_norm(rows):
    mean = jnp.mean(rows, axis=-1, keepdims=True)
    centered = rows - mean
    inv_std = lax.rsqrt(jnp.mean(centered * centered, axis=-1, keepdims=True) + norm_eps)
    return centered * inv_std, inv_std


def row_norm_backward(normed, inv_std, grad):
    mean_grad = jnp.mean(grad, axis=-1, keepdims=True)
    mean_mix = jnp.mean(grad * normed, axis=-1, keepdims=True)
    return inv_std * (grad - mean_grad - normed * mean_mix)


def add_parts(parts_ref):
    total = parts_ref[0].astype(F32)
    for index in range(1, parts_ref.shape[0]):
        total = total + parts_ref[index].astype(F32)
    return total


def fill_copies(copies_ref, rows):
    for index in range(copies_ref.shape[0]):
        copies_ref[index] = rows


def first_norm_body(in_ref, copies_ref):
    normed, _ = row_norm(in_ref[...].astype(F32))
    fill_copies(copies_ref, normed.astype(BF16))


def second_norm_body(parts_ref, in_ref, resid_ref, copies_ref):
    total = add_parts(parts_ref)
    resid = (in_ref[...].astype(F32) + total).astype(BF16)
    resid_ref[...] = resid
    normed, _ = row_norm(resid.astype(F32))
    fill_copies(copies_ref, normed.astype(BF16))


def resid_grad_body(parts_ref, resid_ref, cot_ref, grad_ref, copies_ref, mark_ref):
    mark_ref[...] = jnp.zeros_like(mark_ref)
    total = add_parts(parts_ref)
    normed, inv_std = row_norm(resid_ref[...].astype(F32))
    grad = row_norm_backward(normed, inv_std, total)
    grad = (cot_ref[...].astype(F32) + grad).astype(BF16)
    grad_ref[...] = grad
    fill_copies(copies_ref, grad)


def input_grad_body(
    parts_ref, in_ref, grad_ref, resid_ref, near_ref, far_ref, out_ref, block_ref, wait
):
    total = add_parts(parts_ref)
    wait()
    ffn = near_ref[...].astype(F32) + far_ref[...].astype(F32)
    block_ref[...] = (resid_ref[...].astype(F32) + ffn).astype(BF16)
    normed, inv_std = row_norm(in_ref[...].astype(F32))
    grad = row_norm_backward(normed, inv_std, total)
    out_ref[...] = (grad_ref[...].astype(F32) + grad).astype(BF16)


def pack_place(slot, half_rows):
    image, head, half = slot // 4, (slot // 2) % 2, slot % 2
    row = image * 2 * half_rows
    return row, row + half * half_rows, head * HD


def join_halves(mine_ref, other_ref, rows_ref):
    half = mine_ref.shape[0]
    rows_ref[:half] = mine_ref[...]
    rows_ref[half:] = other_ref[...]


def qkv_body(mine_ref, other_ref, w_ref, send_ref, rows_ref, pack_ref, sems):
    join_halves(mine_ref, other_ref, rows_ref)
    half_rows = pack_ref.shape[1] // 5
    moves = []
    for part in range(3):
        acc = dot(rows_ref[...], w_ref[part]).astype(BF16)
        start = half_rows * max(2 * part - 1, 0)
        size = half_rows * min(part + 1, 2)
        for slot in range(8):
            image_row, row, col = pack_place(slot, half_rows)
            first = row if part == 0 else image_row
            pack_ref[slot, start : start + size] = acc[first : first + size, col : col + HD]
        place = pl.ds(start, size)
        moves.append(
            pltpu.make_async_copy(pack_ref.at[:, place], send_ref.at[:, place], sems.at[part])
        )
        moves[-1].start()
    for move in moves:
        move.wait()


def attention_body(pack_ref, att_ref, lse_ref):
    half_rows = att_ref.shape[1]
    keys = pack_ref[:, half_rows : 3 * half_rows, :].reshape(-1, HD)
    values = pack_ref[:, 3 * half_rows :, :].reshape(-1, HD)
    scale = 1.0 / math.sqrt(HD)
    for chunk in range(4):
        queries = pack_ref[2 * chunk : 2 * chunk + 2, :half_rows, :].reshape(-1, HD)
        scores = dot(keys, queries, NT) * scale
        row_max = jnp.max(scores, axis=0, keepdims=True)
        weights = jnp.exp(scores - row_max)
        total = jnp.sum(weights, axis=0, keepdims=True)
        lse_ref[chunk] = row_max + jnp.log(total)
        mixed = dot(values, weights.astype(BF16), TN) / total
        att_ref[2 * chunk : 2 * chunk + 2] = mixed.T.astype(BF16).reshape(2, half_rows, HD)


def attention_grad_body(pack_ref, att_ref, lse_ref, grad_ref, send_ref, out_ref, sems):
    half_rows = att_ref.shape[1]
    scale = 1.0 / math.sqrt(HD)
    queries = pack_ref[:, :half_rows, :].reshape(-1, HD)
    grads = grad_ref[...].reshape(-1, HD)
    mix = grads.astype(F32) * att_ref[...].reshape(-1, HD).astype(F32)
    delta = jnp.sum(mix.T, axis=0, keepdims=True)
    lse = jnp.concatenate([lse_ref[chunk] for chunk in range(4)], axis=1)
    query_total = None
    moves = []
    for slot in range(8):
        keys = pack_ref[slot, half_rows : 3 * half_rows, :]
        values = pack_ref[slot, 3 * half_rows :, :]
        probs = jnp.exp(dot(keys, queries, NT) * scale - lse)
        grad_probs = dot(values, grads, NT)
        grad_scores = (probs * (grad_probs - delta) * scale).astype(BF16)
        out_ref[slot, half_rows : 3 * half_rows] = dot(grad_scores, queries).astype(BF16)
        out_ref[slot, 3 * half_rows :] = dot(probs.astype(BF16), grads).astype(BF16)
        term = dot(keys, grad_scores, TN)
        query_total = term if query_total is None else query_total + term
        part = pl.ds(half_rows, 4 * half_rows)
        moves.append(
            pltpu.make_async_copy(
                out_ref.at[slot, part], send_ref.at[slot, part], sems.at[slot]
            )
        )
        moves[-1].start()
    out_ref[:, :half_rows] = query_total.T.astype(BF16).reshape(8, half_rows, HD)
    part = pl.ds(0, half_rows)
    moves.append(pltpu.make_async_copy(out_ref.at[:, part], send_ref.at[:, part], sems.at[8]))
    moves[-1].start()
    for move in moves:
        move.wait()


def put_halves(own_ref, other_ref, cols, total):
    half = own_ref.shape[0]
    own_ref[:, cols] = total[:half].astype(BF16)
    other_ref[:, cols] = total[half:].astype(BF16)


def out_body(start, att_ref, w_ref, own_ref, other_ref, rows_ref):
    half_rows = att_ref.shape[1]
    for slot in range(8):
        _, row, col = pack_place(slot, half_rows)
        rows_ref[row : row + half_rows, col : col + HD] = att_ref[slot]
    size = 512
    for step in range(own_ref.shape[1] // size):
        cols = slice(start + step * size, start + (step + 1) * size)
        total = dot(rows_ref[...], w_ref[:, cols])
        put_halves(own_ref, other_ref, slice(step * size, (step + 1) * size), total)


def join_low_body(*refs):
    *block_refs, _, out_ref, sems = refs
    count = len(block_refs)
    low = lax.rem(lax.axis_index("mp"), count)
    high = lax.axis_index("mp") // count
    rows = block_refs[0].shape[1]
    moves = []
    for step in range(count):
        source = lax.rem(low + count - step, count)
        for side, place in ((0, high), (1, 1 - high)):
            start = pl.multiple_of((place * count + source) * rows, rows)
            moves.append(
                pltpu.make_async_copy(
                    block_refs[step].at[side], out_ref.at[pl.ds(start, rows)], sems.at[step, side]
                )
            )
    for move in moves:
        move.start()
    for move in moves:
        move.wait()


def join_low(blocks, after, shape):
    any_spec = pl.BlockSpec(memory_space=pl.ANY)
    return pl.pallas_call(
        join_low_body,
        name="join_cotangent",
        in_specs=[any_spec] * (len(blocks) + 1),
        out_specs=any_spec,
        out_shape=jax.ShapeDtypeStruct(shape, BF16),
        scratch_shapes=[pltpu.SemaphoreType.DMA((len(blocks), 2))],
        compiler_params=pltpu.CompilerParams(vmem_limit_bytes=1024 * 1024),
    )(*[hbm(block) for block in blocks], after)


def split_low_body(own_ref, other_ref, *out_refs):
    count = len(out_refs)
    low = lax.rem(lax.axis_index("mp"), count)
    high = lax.axis_index("mp") // count
    rows = out_refs[0].shape[1]
    for step in range(count):
        target = lax.rem(low + step, count)
        for side, place in ((0, high), (1, 1 - high)):
            start = pl.multiple_of((place * count + target) * rows, rows)
            total = own_ref[pl.ds(start, rows)].astype(F32) + other_ref[pl.ds(start, rows)].astype(F32)
            out_refs[step][side] = total.astype(BF16)


def sum_low_body(*refs):
    near_ref, far_ref = refs[-2:]
    for side, out_ref in enumerate((near_ref, far_ref)):
        total = refs[0][side].astype(F32)
        for ref in refs[1:-2]:
            total = total + ref[side].astype(F32)
        out_ref[...] = total.astype(BF16)


def grad_act_body(mine_ref, other_ref, w_ref, out_ref, rows_ref):
    @pl.when(pl.program_id(0) == 0)
    def _():
        join_halves(mine_ref, other_ref, rows_ref)

    out_ref[...] = dot(rows_ref[...], w_ref[...], NT)


def hidden_body(
    mine_ref, other_ref, w_ref, act_ref, hidden_ref, grad_ref, rows_ref
):
    join_halves(mine_ref, other_ref, rows_ref)

    for step in range(w_ref.shape[1] // 256):
        cols = slice(step * 256, (step + 1) * 256)
        pre = dot(rows_ref[...], w_ref[:, cols])
        cumul = 0.5 * (1.0 + lax.erf(pre * 0.7071067811865476))
        hidden_ref[:, cols] = (pre * cumul).astype(BF16)
        slope = cumul + pre * jnp.exp(-0.5 * pre * pre) * 0.3989422804014327
        grad_ref[:, cols] = (act_ref[:, cols] * slope).astype(BF16)


def grad_norm_body(start, rows_ref, w_ref, own_ref, other_ref):
    size = 512
    for step in range(own_ref.shape[1] // size):
        source = slice(start + step * size, start + (step + 1) * size)
        total = dot(rows_ref[...], w_ref[source, :], NT)
        put_halves(own_ref, other_ref, slice(step * size, (step + 1) * size), total)


def pair_body(*refs):
    *sides, out_ref, total_ref, sems = refs
    size = sides[0].shape[1]
    count = sems.shape[0]
    rows = out_ref.shape[0] // count
    moves = []
    for step in range(count):
        part = pl.ds(step * rows, rows)
        for index in range(len(sides) // 2):
            total = sides[2 * index][part].astype(F32) + sides[2 * index + 1][part].astype(F32)
            total_ref[part, index * size : (index + 1) * size] = total.astype(BF16)
        moves.append(
            pltpu.make_async_copy(total_ref.at[part], out_ref.at[part], sems.at[step])
        )
        moves[-1].start()
    for move in moves:
        move.wait()


def down_body(rows_ref, w_ref, own_ref, other_ref):
    put_halves(own_ref, other_ref, slice(None), dot(rows_ref[...], w_ref[...]))


def out_grad_body(mine_ref, other_ref, w_ref, pack_ref, rows_ref):
    join_halves(mine_ref, other_ref, rows_ref)
    half_rows = pack_ref.shape[1]
    grad = dot(rows_ref[...], w_ref[...], NT).astype(BF16)
    for slot in range(8):
        _, row, col = pack_place(slot, half_rows)
        pack_ref[slot] = grad[row : row + half_rows, col : col + HD]


def qkv_grad_body(base, pack_ref, w_ref, *refs):
    own_ref, other_ref, rows_ref, w_buf, sems = refs[-5:]
    half_rows = pack_ref.shape[1] // 5
    steps = sems.shape[0]
    size = w_buf.shape[1] // steps

    def move(step):
        source = pl.ds(base + step * size, size)
        cols = pl.ds(step * size, size)
        return pltpu.make_async_copy(w_ref.at[:, source, :], w_buf.at[:, cols, :], sems.at[step])

    for step in range(steps):
        move(step).start()
    for slot in range(8):
        _, row, col = pack_place(slot, half_rows)
        rows_ref[0, row : row + half_rows, col : col + HD] = pack_ref[slot, :half_rows]
    for slot in range(0, 8, 2):
        row, _, col = pack_place(slot, half_rows)
        for part in (1, 2):
            start = half_rows * (2 * part - 1)
            both = pack_ref[slot, start : start + 2 * half_rows].astype(F32) + pack_ref[
                slot + 1, start : start + 2 * half_rows
            ].astype(F32)
            rows_ref[part, row : row + 2 * half_rows, col : col + HD] = both.astype(BF16)

    for step in range(steps):
        move(step).wait()
        cols = slice(step * size, (step + 1) * size)
        total = dot(rows_ref[0], w_buf[0, cols, :], NT)
        for part in (1, 2):
            total = total + dot(rows_ref[part], w_buf[part, cols, :], NT)
        put_halves(own_ref, other_ref, cols, total)


def swap_section(data):
    return lax.ppermute(data, "section", [(0, 1), (1, 0)])


def exchange(data, axis):
    return lax.all_to_all(data, axis, 0, 0)


def by_columns(partial, half, width, hold=None):
    sides = [partial(start) for start in (0, width // 2)]
    if hold is not None:
        own, other = sides[0]
        other, hold[0] = lax.optimization_barrier((other, hold[0]))
        sides[0] = own, other
    ins = []
    for own, other in sides:
        ins += [own, swap_section(other)]
    return pl.pallas_call(
        pair_body,
        name="pair",
        in_specs=[pl.BlockSpec(memory_space=pltpu.VMEM)] * len(ins),
        out_specs=pl.BlockSpec(memory_space=pl.ANY),
        out_shape=jax.ShapeDtypeStruct((half, width), BF16),
        scratch_shapes=[pltpu.VMEM((half, width), BF16), pltpu.SemaphoreType.DMA((4,))],
        compiler_params=pltpu.CompilerParams(vmem_limit_bytes=16 * 1024 * 1024),
    )(*ins)


def pair_sum(own, other):
    return (own.astype(F32) + swap_section(other).astype(F32)).astype(BF16)


def shift_high(data):
    size = lax.axis_size("mp")
    return lax.ppermute(data, "mp", [(i, (i + size // 2) % size) for i in range(size)])


def shift_low(data, step):
    size = lax.axis_size("mp") // 2
    pairs = [(h * size + i, h * size + (i + step) % size) for h in range(2) for i in range(size)]
    return lax.ppermute(data, "mp", pairs)


def per_device(bottleneck, qkv_weight, out_weight, up_weight, down_weight, cotangent):
    own_in = bottleneck[0]
    own_cot = cotangent[0]
    rows, width = own_in.shape
    group = lax.axis_size("mp")
    seq_size = lax.axis_size("seq")
    half = rows * group
    total_rows = 2 * half
    half_rows = half // 2
    head_cols = qkv_weight.shape[2]
    units = up_weight.shape[1]
    assert (total_rows // half) * (head_cols // HD) * 2 == seq_size == 8
    copies = ((group, rows, width), BF16)
    row_out = ((rows, width), BF16)
    halves = [((half, width), BF16)] * 2
    column_halves = [((half, width // 2), BF16)] * 2
    att_shape = ((seq_size, half_rows, HD), BF16)
    pack_shape = ((seq_size, 5 * half_rows, HD), BF16)
    big = 2 * total_rows * width * units
    joined = pltpu.VMEM((total_rows, width), BF16)

    (send,) = local_call(first_norm_body, "first_norm", [own_in], [copies])
    send, cot_near = lax.optimization_barrier((send, own_cot))
    cot_far = shift_high(cot_near)
    weight = fetch(qkv_weight, send, "fetch_qkv")
    mine, cot_far = lax.optimization_barrier((exchange(send, "mp"), cot_far))
    mine = mine.reshape(half, width)
    (send,) = local_call(
        qkv_body,
        "qkv",
        [mine, swap_section(mine), weight],
        [pack_shape + ("hbm",)],
        [joined, pltpu.VMEM(*pack_shape), pltpu.SemaphoreType.DMA((3,))],
        flops=2 * total_rows * width * 3 * head_cols,
    )
    send, cot_near, cot_far = lax.optimization_barrier((send, cot_near, cot_far))
    cot_two = jnp.stack([cot_near, cot_far])
    pack = exchange(send, "seq")
    cot_shifted = [shift_low(cot_two, step) for step in range(1, group // 2)]
    att, lse = local_call(
        attention_body,
        "attention",
        [pack],
        [att_shape, ((4, 1, 2 * half_rows), F32)],
        flops=4 * half * half * 8 * HD,
    )
    weight = fetch(out_weight, att, "fetch_out")
    got = exchange(att, "seq")
    cot_mine = join_low([cot_two, *cot_shifted], att, (half, width))
    cots = [cot_mine, swap_section(cot_mine)]

    def attn_out(start):
        return local_call(
            functools.partial(out_body, start),
            "attn_out",
            [got, weight],
            column_halves,
            [pltpu.VMEM((total_rows, head_cols), BF16)],
            after=[cot_mine],
        )

    send = by_columns(attn_out, half, width).reshape(group, rows, width)
    unit_block = units // 4
    unit_spec = pl.BlockSpec((total_rows, unit_block), lambda j: (0, j))
    (grad_act,) = kernel_call(
        grad_act_body,
        "grad_act",
        (4,),
        [
            *[(cot, None) for cot in cots],
            (hbm(down_weight), pl.BlockSpec((unit_block, width), lambda j: (j, 0))),
        ],
        [((total_rows, units), F32, unit_spec)],
        [joined],
        after=[send],
        flops=big,
        nbytes=2 * width * units,
    )
    parts = exchange(send, "mp")
    resid, send = local_call(
        second_norm_body, "second_norm", [parts, own_in], [row_out, copies], after=[grad_act]
    )
    mine = exchange(send, "mp").reshape(half, width)
    weight = fetch(up_weight, send, "fetch_up")
    hidden, grad_hidden = local_call(
        hidden_body,
        "hidden",
        [mine, swap_section(mine), weight, grad_act],
        [((total_rows, units), BF16)] * 2,
        [joined],
        flops=big,
    )

    def grad_norm_two(start):
        return local_call(
            functools.partial(grad_norm_body, start),
            "grad_norm_two",
            [grad_hidden, weight],
            column_halves,
        )

    send = by_columns(grad_norm_two, half, width).reshape(group, rows, width)
    block = width // 8
    block_spec = pl.BlockSpec((half, block), lambda j: (0, j))
    own, other = kernel_call(
        down_body,
        "down",
        (8,),
        [(hidden, None), (hbm(down_weight), pl.BlockSpec((units, block), lambda j: (0, j)))],
        [(shape, dtype, block_spec) for shape, dtype in halves],
        after=[send],
        flops=big,
        nbytes=2 * width * units,
    )
    parts = exchange(send, "mp")
    grad_resid, send, mark = local_call(
        resid_grad_body,
        "resid_grad",
        [parts, resid, own_cot],
        [row_out, copies, ((8, 128), F32)],
        after=[own],
    )
    weight = fetch(out_weight, send, "fetch_out_again")
    other, mark = lax.optimization_barrier((other, mark))
    sums_low = local_call(
        split_low_body,
        "split_sums",
        [own, swap_section(other)],
        [((2, rows, width), BF16)] * (group // 2),
    )
    mine, *sums_low = lax.optimization_barrier((exchange(send, "mp"), *sums_low))
    mine = mine.reshape(half, width)
    (send,) = local_call(
        out_grad_body,
        "attn_out_grad",
        [mine, swap_section(mine), weight],
        [att_shape],
        [joined],
        after=[mark],
        flops=2 * total_rows * width * head_cols,
    )
    grad_att = exchange(send, "seq")
    (send,) = local_call(
        attention_grad_body,
        "attention_grad",
        [pack, att, lse, grad_att],
        [pack_shape + ("hbm",)],
        [pltpu.VMEM(*pack_shape), pltpu.SemaphoreType.DMA((9,))],
        flops=10 * half * half * 8 * HD,
    )
    send, *sums_low = lax.optimization_barrier((send, *sums_low))
    shifted = [shift_low(sums_low[step], step) for step in range(1, group // 2)]
    sum_near, sum_far = local_call(
        sum_low_body, "join_sums", [sums_low[0], *shifted], [row_out] * 2
    )
    sum_far = shift_high(sum_far)
    got = exchange(send, "seq")
    vmem = pl.BlockSpec(memory_space=pltpu.VMEM)
    hold = [sum_far]

    def qkv_grad(start):
        after = shifted if start == 0 else [sum_near]
        return pl.pallas_call(
            functools.partial(qkv_grad_body, start),
            name="qkv_grad",
            in_specs=[vmem, pl.BlockSpec(memory_space=pltpu.HBM)]
            + [pl.BlockSpec(memory_space=pl.ANY)] * len(after),
            out_specs=[vmem] * 2,
            out_shape=[jax.ShapeDtypeStruct(shape, dtype) for shape, dtype in column_halves],
            scratch_shapes=[
                pltpu.VMEM((3, total_rows, head_cols), BF16),
                pltpu.VMEM((3, width // 2, head_cols), BF16),
                pltpu.SemaphoreType.DMA((4,)),
            ],
            compiler_params=pltpu.CompilerParams(vmem_limit_bytes=16 * 1024 * 1024),
            cost_estimate=pl.CostEstimate(flops=0, bytes_accessed=0, transcendentals=0),
        )(got, hbm(qkv_weight), *after)

    parts = exchange(by_columns(qkv_grad, half, width, hold).reshape(group, rows, width), "mp")
    grad_input, block_out = local_call(
        input_grad_body,
        "input_grad",
        [parts],
        [row_out, row_out],
        late=[hbm(own_in), grad_resid, resid, sum_near, hold[0]],
    )
    return (block_out[None], grad_input[None])


def solution(mesh):
    in_specs = (
        P("section", ("seq", "mp"), None),
        P(None, None, ("section", "mp")),
        P(("section", "mp"), None),
        P(None, ("section", "mp")),
        P(("section", "mp"), None),
        P("section", ("seq", "mp"), None),
    )
    out_specs = (P("section", ("seq", "mp"), None), P("section", ("seq", "mp"), None))
    return jax.shard_map(
        per_device, mesh=mesh, in_specs=in_specs, out_specs=out_specs, check_vma=False
    )
```
